256 devices in a mesh: gx: 16 (over z, core), gy: 4 (over y), gz: 4 (over x).
Axes of the slice: x: 4, y: 4, z: 8, core: 2. Of those that a mesh axis runs over, the one named last changes fastest.
Arguments:
- basis: float32 [32, 2097152], P(None, ('gx', 'gy', 'gz')), may hold values from -5.5 to 5.5
- sigma: float32 [32], replicated, may hold values from 1 to 8
- snapshots: float32 [64, 2097152], P(None, ('gx', 'gy', 'gz')), may hold values from -200 to 200
Outputs:
- modes: float32 [32, 2097152], P(None, ('gx', 'gy', 'gz'))
- values: float32 [32], replicated
The draws below stay inside these ranges and needn't reach their ends.
All inputs are finite; a program needn't handle non-finite values.
Results may differ from the reference program's by a relative error of at most 0.00016.
Values sent between devices are 32-bit elements; how exact they have to be, the bound alone decides.
A program may use at most 64 MiB of HBM per device.

```python
import math
import jax
import jax.numpy as jnp
from jax import lax

K = 32
NEW = 64
ITERS = 4
ROWS = 2097152


def common_basis(key):
    basis_key = jax.random.fold_in(key, 11)
    sample = jnp.clip(jax.random.normal(basis_key, (K, ROWS), jnp.float32), -5.0, 5.0)
    return sample + 0.05 * jnp.roll(sample, 1, axis=0)


def draw_basis(key, part):
    return common_basis(key)


def draw_snapshots(key, part):
    basis = common_basis(key)
    mixing = jax.random.normal(jax.random.fold_in(key, 12), (K, NEW), jnp.float32)
    noise_key = jax.random.fold_in(key, 13)
    spread_key = jax.random.fold_in(key, 14)
    noise = jax.random.normal(noise_key, (NEW, ROWS), jnp.float32)
    spread = jnp.exp(jax.random.uniform(spread_key, (ROWS,), jnp.float32, -0.3566749, 0.3364722))
    place = jnp.arange(ROWS, dtype=jnp.float32) / ROWS
    rising = 0.5 + place
    signal = jnp.dot(mixing.T, basis, precision=lax.Precision.HIGHEST) * rising
    return jnp.clip(signal + 0.5 * spread * noise, -200.0, 200.0)


def setup_inputs(seed: int = 0) -> dict:
    keys = jax.random.split(jax.random.key(seed), 4)
    return {
        "basis": draw_basis(jax.random.fold_in(keys[3], 71), 0),
        "sigma": jnp.clip(jnp.exp(jax.random.uniform(keys[1], (K,), jnp.float32, math.log(1.0), math.log(8.0))), 1.0, 8.0),
        "snapshots": draw_snapshots(jax.random.fold_in(keys[3], 71), 0),
    }


HIGH = lax.Precision.HIGHEST

def inner(left, right, total):
    product = lax.dot_general(left.astype(jnp.float32), right.astype(jnp.float32), (((1,), (1,)), ((), ())), precision=HIGH, preferred_element_type=jnp.float32)
    return product / total

def orthonormal(block):
    for repeat in range(2):
        factor = jnp.linalg.cholesky(jnp.dot(block.T, block, precision=HIGH))
        block = jax.scipy.linalg.solve_triangular(factor, block.T, lower=True).T
    return block

def rotate(sigma, coeffs, factor):
    modes_count = sigma.shape[0]
    fresh_count = factor.shape[0]
    upper_rows = jnp.concatenate([jnp.diag(sigma), coeffs], axis=1)
    lower_rows = jnp.concatenate([jnp.zeros((fresh_count, modes_count), jnp.float32), factor], axis=1)
    core = jnp.concatenate([upper_rows, lower_rows], axis=0)
    square = jnp.dot(core, core.T, precision=HIGH)
    frame = jnp.eye(modes_count + fresh_count, modes_count, dtype=jnp.float32)
    for step in range(ITERS):
        frame = orthonormal(jnp.dot(square, frame, precision=HIGH))
    ritz = lax.optimization_barrier(jnp.sum(frame * jnp.dot(square, frame, precision=HIGH), axis=0))
    return (frame, jnp.sqrt(ritz))

def reference(basis, sigma, snapshots):
    modes_count = basis.shape[0]
    total = basis.shape[1] * 1.0
    first = inner(basis, snapshots, total)
    partial_value = snapshots - jnp.dot(first.T, basis, precision=HIGH)
    second = inner(basis, partial_value, total)
    residual = partial_value - jnp.dot(second.T, basis, precision=HIGH)
    gram = inner(residual, residual, total)
    lower = jnp.linalg.cholesky(gram)
    fresh = jax.scipy.linalg.solve_triangular(lower, residual, lower=True)
    frame, values = rotate(sigma, first + second, lower.T)
    modes = jnp.dot(frame[:modes_count].T, basis, precision=HIGH) + jnp.dot(frame[modes_count:].T, fresh, precision=HIGH)
    return (modes, values)
```

```python
import functools

import jax
import jax.numpy as jnp
from jax import lax
from jax.experimental import pallas as pl
from jax.experimental.pallas import tpu as pltpu
from jax.sharding import PartitionSpec as P

AXES = ("gx", "gy", "gz")
HIGH = lax.Precision.HIGHEST
K, NEW = 32, 64

def dot(a, b): return jnp.dot(a, b, precision=HIGH, preferred_element_type=jnp.float32)
def dot_t(a, b): return lax.dot_general(a, b, (((1,), (1,)), ((), ())), precision=HIGH, preferred_element_type=jnp.float32)

def eliminate(N, U):
    nb = N.shape[0] // 8
    Nb = [N[8*i:8*i+8] for i in range(nb)]
    Ub = [U[8*i:8*i+8] for i in range(nb)]
    row = lax.broadcasted_iota(jnp.int32, (8, 128), 0)
    L = U.shape[1]
    def wide(x, width):
        return x[:, :width] if width <= 128 else jnp.concatenate([x] * (width // 128), axis=1)
    out = []
    for kb in range(nb):
        X = {}
        for j in range(8):
            for i in range(kb, nb):
                X[j, i] = jnp.broadcast_to(Nb[i][:, 8*kb+j:8*kb+j+1], (8, 128))
        scale = jnp.ones((8, 128), jnp.float32)
        for r in range(0, 8, 2):
            spread = lambda x, s: jnp.broadcast_to(x[s:s+1], (8, x.shape[1]))
            a = spread(X[r, kb], r); b = spread(X[r+1, kb], r); c = spread(X[r+1, kb], r+1)
            det = a*c - b*b
            rdet = 1.0 / det
            ra = 1.0 / a
            f1 = {}; f2 = {}
            for i in range(kb, nb):
                f1[i] = (c*X[r, i] - b*X[r+1, i]) * rdet
                f2[i] = (a*X[r+1, i] - b*X[r, i]) * rdet
                if i == kb:
                    f1[i] = jnp.where(row > r+1, f1[i], jnp.where(row == r+1, b*ra, 0.0))
                    f2[i] = jnp.where(row > r+1, f2[i], 0.0)
            for j in range(r+2, 8):
                xa = spread(X[j, kb], r); xb = spread(X[j, kb], r+1)
                for i in range(kb, nb):
                    X[j, i] = X[j, i] - f1[i]*xa - f2[i]*xb
            na = spread(Nb[kb], r); nbb = spread(Nb[kb], r+1)
            ua = spread(Ub[kb], r); ub = spread(Ub[kb], r+1)
            for i in range(kb, nb):
                if kb < nb-1:
                    w = Nb[i].shape[1]
                    Nb[i] = Nb[i] - wide(f1[i], w)*na - wide(f2[i], w)*nbb
                Ub[i] = Ub[i] - wide(f1[i], L)*ua - wide(f2[i], L)*ub
            scale = jnp.where(row == r, lax.rsqrt(a), jnp.where(row == r+1, lax.rsqrt(det*ra), scale))
        out.append(Ub[kb] * wide(scale, L))
    return jnp.concatenate(out, axis=0)

def dense(gbb, f, gss, sigma_row):
    ft = f.T
    t = dot(gbb, f)
    c = 2.0*f - t
    ct = 2.0*ft - dot(ft, gbb)
    h = dot(gbb, c) - f
    gram = gss + dot(jnp.concatenate([ct, -ft], 1), jnp.concatenate([h, c], 0))
    eye = lax.broadcasted_iota(jnp.int32, (K, K), 0) == lax.broadcasted_iota(jnp.int32, (K, K), 1)
    eye2 = lax.broadcasted_iota(jnp.int32, (NEW, NEW), 0) == lax.broadcasted_iota(jnp.int32, (NEW, NEW), 1)
    tau = jnp.sum(c*c, keepdims=True).reshape(1,1) + jnp.sum(jnp.where(eye2, gss, 0.0), keepdims=True).reshape(1,1) + jnp.sum(sigma_row*sigma_row, keepdims=True).reshape(1,1)
    rt = 1.0 / tau
    rs = lax.rsqrt(tau)
    sig2 = jnp.where(eye, sigma_row*sigma_row, 0.0)
    p = (sig2 + dot_t(c, c)) * rt
    cu = c
    c = c*rs; ct = ct*rs; gram = gram*rt
    cg = dot(c, gram); cgt = dot(gram, ct); g2 = dot(gram, gram)
    z32 = jnp.zeros((K, 32), jnp.float32); z64 = jnp.zeros((NEW, 32), jnp.float32)
    top = jnp.concatenate([p, c, z32, p, cg, z32], 1)
    bot = jnp.concatenate([cgt, gram, z64, cgt, g2, z64], 1)
    W = jnp.concatenate([top, bot], 0)
    VZ = top
    for step in range(4):
        V = VZ[:, :96]; Z = VZ[:, 128:224]
        N = dot_t(Z, V)
        VZ = eliminate(N, dot(V, W) if step < 3 else VZ)
    Y = VZ[:, :128]
    P = Y[:, :32]; w = Y[:, 32:96]
    Z = jnp.concatenate([P, dot(w, gram), z32], 1)
    N = dot_t(Z, Y)
    YS = dot(Y[:, :96], W[:, 128:])
    pb = P - dot(w, ct)
    U = jnp.concatenate([pb, w*rs, z32, Y, YS], 1)
    U = eliminate(N, U)
    ritz = jnp.sum(U[:, 128:224] * U[:, 256:352], axis=1, keepdims=True)
    values = jnp.sqrt(ritz * tau)
    return U[:, :128], values


CHUNK = 2048


def gram_kernel(na, ny, nz, basis_hbm, snap_hbm, total_ref, split_hbm,
                basis_v, snap_v, split_v, packed, parts, mine, others, gathered,
                load_sems, store_sem, send_sems, recv_sems):
    x, y, z = lax.axis_index("gx"), lax.axis_index("gy"), lax.axis_index("gz")
    count = ny * nz
    cols = basis_v.shape[1]
    chunks = cols // CHUNK
    loads = []
    for i in range(chunks):
        at = pl.ds(i * CHUNK, CHUNK)
        loads.append((
            pltpu.make_async_copy(basis_hbm.at[:, at], basis_v.at[:, at], load_sems.at[0, i]),
            pltpu.make_async_copy(snap_hbm.at[:, at], snap_v.at[:, at], load_sems.at[1, i]),
        ))
        for copy in loads[-1]:
            copy.start()

    barrier = pltpu.get_barrier_semaphore()
    for d in range(1, na):
        pl.semaphore_signal(barrier, inc=1, device_id={"gx": lax.rem(x + d, na)}, device_id_type=pl.DeviceIdType.MESH)
    def place(d):
        return {"gy": lax.rem(y + d // nz, ny), "gz": lax.rem(z + d % nz, nz)}
    for d in range(1, count):
        pl.semaphore_signal(barrier, inc=1, device_id=place(d), device_id_type=pl.DeviceIdType.MESH)

    full = None
    for i in range(chunks):
        for copy in loads[i]:
            copy.wait()
        at = slice(i * CHUNK, (i + 1) * CHUNK)
        for ref, low in ((basis_v, 0), (snap_v, K)):
            value = ref[:, at]
            high = value.astype(jnp.bfloat16)
            rest = (value - high.astype(jnp.float32)).astype(jnp.bfloat16)
            split_v[low:low + value.shape[0], at] = high
            split_v[K + NEW + low:K + NEW + low + value.shape[0], at] = rest
        pair = split_v[:, at]
        term = lax.dot_general(pair, pair, (((1,), (1,)), ((), ())), preferred_element_type=jnp.float32)
        full = term if full is None else full + term
    store = pltpu.make_async_copy(split_v, split_hbm, store_sem)
    store.start()
    half = K + NEW
    gram = (full[:half, :half] + full[half:, half:]) + (full[half:, :half] + full[:half, half:])
    gap = jnp.zeros((K, 128 - half), jnp.float32)
    upper = jnp.concatenate([gram[:K], gap], axis=1)
    lower = jnp.concatenate([gram[K:2 * K, K:], gram[2 * K:, K:]], axis=1)
    rows = packed.shape[1]
    both = jnp.concatenate([upper, lower], axis=0)
    for i in range(na):
        packed[i] = both[i * rows:(i + 1) * rows]

    pl.semaphore_wait(barrier, na - 1 + count - 1)

    def send(phase, source, target, device):
        copy = pltpu.make_async_remote_copy(
            src_ref=source, dst_ref=target, send_sem=send_sems.at[phase], recv_sem=recv_sems.at[phase],
            device_id=device, device_id_type=pl.DeviceIdType.MESH)
        copy.start()

    def arrive(phase, ref):
        pltpu.make_async_copy(ref, ref, recv_sems.at[phase]).wait()

    def sent(phase, ref):
        pltpu.make_async_copy(ref, ref, send_sems.at[phase]).wait()

    for d in range(1, na):
        to = lax.rem(x + d, na)
        send(0, packed.at[to], parts.at[d - 1], {"gx": to})
    arrive(0, parts)
    value = packed[x]
    for d in range(na - 1):
        value = value + parts[d]
    mine[...] = value

    here = y * nz + z
    for d in range(1, count):
        send(1, mine, others.at[here], place(d))
    others[here] = value
    arrive(1, others.at[pl.ds(0, count - 1)])
    value = others[0]
    for d in range(1, count):
        value = value + others[d]
    gathered[x] = value

    for d in range(1, na):
        send(2, gathered.at[x], gathered.at[x], {"gx": lax.rem(x + d, na)})
    arrive(2, gathered.at[pl.ds(0, na - 1)])
    for i in range(na):
        total_ref[i] = gathered[i]
    sent(0, parts)
    sent(1, others.at[pl.ds(0, count - 1)])
    sent(2, gathered.at[pl.ds(0, na - 1)])
    store.wait()


def update_kernel(rows, total_ref, sigma_ref, split_hbm, modes_ref, values_ref, split_v, sem):
    cols = split_v.shape[1]
    copy = pltpu.make_async_copy(split_hbm, split_v, sem)
    copy.start()
    total = total_ref[...] * (1.0 / rows)
    upper, lower = total[:K], total[K:]
    gss = jnp.concatenate([lower[:, :NEW], lower[:, NEW:]], axis=0)
    coef, values = dense(upper[:, :K], upper[:, K:K + NEW], gss, sigma_ref[...])
    eye = lax.broadcasted_iota(jnp.int32, (K, K), 0) == lax.broadcasted_iota(jnp.int32, (K, K), 1)
    values_ref[...] = jnp.sum(jnp.where(eye, values, 0.0), axis=0, keepdims=True)
    coef = coef[:, :K + NEW]
    high = coef.astype(jnp.bfloat16).astype(jnp.float32)
    rest = coef - high
    left = jnp.concatenate([
        jnp.concatenate([high, high], axis=1), jnp.concatenate([rest, rest], axis=1)], axis=0).astype(jnp.bfloat16)
    copy.wait()
    for i in range(cols // CHUNK):
        at = slice(i * CHUNK, (i + 1) * CHUNK)
        both = jnp.dot(left, split_v[:, at], preferred_element_type=jnp.float32)
        modes_ref[:, at] = both[:K] + both[K:]


def per_device(basis, sigma, snapshots):
    na, ny, nz = (lax.axis_size(a) for a in AXES)
    cols = basis.shape[1]
    rows = cols * na * ny * nz
    piece = 2 * K // na
    vmem = pl.BlockSpec(memory_space=pltpu.VMEM)
    hbm = pl.BlockSpec(memory_space=pl.ANY)
    count = ny * nz
    total, split = pl.pallas_call(
        functools.partial(gram_kernel, na, ny, nz),
        out_shape=(jax.ShapeDtypeStruct((na, piece, 128), jnp.float32),
                   jax.ShapeDtypeStruct((2 * (K + NEW), cols), jnp.bfloat16)),
        in_specs=[hbm, hbm],
        out_specs=(vmem, hbm),
        scratch_shapes=[
            pltpu.VMEM((K, cols), jnp.float32),
            pltpu.VMEM((NEW, cols), jnp.float32),
            pltpu.VMEM((2 * (K + NEW), cols), jnp.bfloat16),
            pltpu.VMEM((na, piece, 128), jnp.float32),
            pltpu.VMEM((na - 1, piece, 128), jnp.float32),
            pltpu.VMEM((piece, 128), jnp.float32),
            pltpu.VMEM((count, piece, 128), jnp.float32),
            pltpu.VMEM((na, piece, 128), jnp.float32),
            pltpu.SemaphoreType.DMA((2, cols // CHUNK)),
            pltpu.SemaphoreType.DMA,
            pltpu.SemaphoreType.DMA((3,)),
            pltpu.SemaphoreType.DMA((3,)),
        ],
        compiler_params=pltpu.CompilerParams(
            collective_id=0, has_side_effects=True, vmem_limit_bytes=32 * 1024 * 1024),
        name="gram_reduce",
    )(basis, snapshots)
    modes, values = pl.pallas_call(
        functools.partial(update_kernel, rows),
        out_shape=(jax.ShapeDtypeStruct((K, cols), jnp.float32),
                   jax.ShapeDtypeStruct((1, K), jnp.float32)),
        in_specs=[vmem, vmem, hbm],
        out_specs=(vmem, vmem),
        scratch_shapes=[pltpu.VMEM((2 * (K + NEW), cols), jnp.bfloat16), pltpu.SemaphoreType.DMA],
        compiler_params=pltpu.CompilerParams(vmem_limit_bytes=32 * 1024 * 1024),
        name="modes_update",
    )(total.reshape(2 * K, 128), sigma.reshape(1, K), split)
    return modes, values.reshape(K)


def solution(mesh):
    placed = (P(None, AXES), P(), P(None, AXES))
    return jax.shard_map(
        per_device, mesh=mesh, in_specs=placed, out_specs=(P(None, AXES), P()), check_vma=False)
```

```python
import functools

import jax
import jax.numpy as jnp
from jax import lax
from jax.experimental import pallas as pl
from jax.experimental.pallas import tpu as pltpu
from jax.sharding import PartitionSpec as P

AXES = ("gx", "gy", "gz")
MESH = pl.DeviceIdType.MESH
HIGH = lax.Precision.HIGHEST
K, NEW = 32, 64

def dot(a, b): return jnp.dot(a, b, precision=HIGH, preferred_element_type=jnp.float32)
def dot_t(a, b): return lax.dot_general(a, b, (((1,), (1,)), ((), ())), precision=HIGH, preferred_element_type=jnp.float32)

def eliminate(N, U):
    nb = N.shape[0] // 8
    Nb = [N[8*i:8*i+8] for i in range(nb)]
    Ub = [U[8*i:8*i+8] for i in range(nb)]
    row = lax.broadcasted_iota(jnp.int32, (8, 128), 0)
    L = U.shape[1]
    def wide(x, width):
        return x[:, :width] if width <= 128 else jnp.concatenate([x] * (width // 128), axis=1)
    out = []
    for kb in range(nb):
        X = {}
        for j in range(8):
            for i in range(kb, nb):
                X[j, i] = jnp.broadcast_to(Nb[i][:, 8*kb+j:8*kb+j+1], (8, 128))
        scale = jnp.ones((8, 128), jnp.float32)
        for r in range(0, 8, 2):
            spread = lambda x, s: jnp.broadcast_to(x[s:s+1], (8, x.shape[1]))
            a = spread(X[r, kb], r); b = spread(X[r+1, kb], r); c = spread(X[r+1, kb], r+1)
            det = a*c - b*b
            rdet = 1.0 / det
            ra = 1.0 / a
            f1 = {}; f2 = {}
            for i in range(kb, nb):
                f1[i] = (c*X[r, i] - b*X[r+1, i]) * rdet
                f2[i] = (a*X[r+1, i] - b*X[r, i]) * rdet
                if i == kb:
                    f1[i] = jnp.where(row > r+1, f1[i], jnp.where(row == r+1, b*ra, 0.0))
                    f2[i] = jnp.where(row > r+1, f2[i], 0.0)
            for j in range(r+2, 8):
                xa = spread(X[j, kb], r); xb = spread(X[j, kb], r+1)
                for i in range(kb, nb):
                    X[j, i] = X[j, i] - f1[i]*xa - f2[i]*xb
            na = spread(Nb[kb], r); nbb = spread(Nb[kb], r+1)
            ua = spread(Ub[kb], r); ub = spread(Ub[kb], r+1)
            for i in range(kb, nb):
                if kb < nb-1:
                    w = Nb[i].shape[1]
                    Nb[i] = Nb[i] - wide(f1[i], w)*na - wide(f2[i], w)*nbb
                Ub[i] = Ub[i] - wide(f1[i], L)*ua - wide(f2[i], L)*ub
            scale = jnp.where(row == r, lax.rsqrt(a), jnp.where(row == r+1, lax.rsqrt(det*ra), scale))
        out.append(Ub[kb] * wide(scale, L))
    return jnp.concatenate(out, axis=0)

def dense(gbb, f, gss, sigma_row):
    ft = f.T
    t = dot(gbb, f)
    c = 2.0*f - t
    ct = 2.0*ft - dot(ft, gbb)
    h = dot(gbb, c) - f
    gram = gss + dot(jnp.concatenate([ct, -ft], 1), jnp.concatenate([h, c], 0))
    eye = lax.broadcasted_iota(jnp.int32, (K, K), 0) == lax.broadcasted_iota(jnp.int32, (K, K), 1)
    eye2 = lax.broadcasted_iota(jnp.int32, (NEW, NEW), 0) == lax.broadcasted_iota(jnp.int32, (NEW, NEW), 1)
    tau = jnp.sum(c*c, keepdims=True).reshape(1,1) + jnp.sum(jnp.where(eye2, gss, 0.0), keepdims=True).reshape(1,1) + jnp.sum(sigma_row*sigma_row, keepdims=True).reshape(1,1)
    rt = 1.0 / tau
    rs = lax.rsqrt(tau)
    sig2 = jnp.where(eye, sigma_row*sigma_row, 0.0)
    p = (sig2 + dot_t(c, c)) * rt
    cu = c
    c = c*rs; ct = ct*rs; gram = gram*rt
    cg = dot(c, gram); cgt = dot(gram, ct); g2 = dot(gram, gram)
    z32 = jnp.zeros((K, 32), jnp.float32); z64 = jnp.zeros((NEW, 32), jnp.float32)
    top = jnp.concatenate([p, c, z32, p, cg, z32], 1)
    bot = jnp.concatenate([cgt, gram, z64, cgt, g2, z64], 1)
    W = jnp.concatenate([top, bot], 0)
    VZ = top
    for step in range(4):
        V = VZ[:, :96]; Z = VZ[:, 128:224]
        N = dot_t(Z, V)
        VZ = eliminate(N, dot(V, W) if step < 3 else VZ)
    Y = VZ[:, :128]
    P = Y[:, :32]; w = Y[:, 32:96]
    Z = jnp.concatenate([P, dot(w, gram), z32], 1)
    N = dot_t(Z, Y)
    YS = dot(Y[:, :96], W[:, 128:])
    pb = P - dot(w, ct)
    U = jnp.concatenate([pb, w*rs, z32, Y, YS], 1)
    U = eliminate(N, U)
    ritz = jnp.sum(U[:, 128:224] * U[:, 256:352], axis=1, keepdims=True)
    values = jnp.sqrt(ritz * tau)
    return U[:, :128], values


CHUNK = 2048
STACK = 2 * (K + NEW)


def tree_sum(values):
    while len(values) > 1:
        values = [a + b for a, b in zip(values[::2], values[1::2])] + values[len(values) // 2 * 2:]
    return values[0]


def split_gram(loads, basis_v, snap_v, split_v):
    full = None
    for i, pair in enumerate(loads):
        for copy in pair:
            copy.wait()
        at = slice(i * CHUNK, (i + 1) * CHUNK)
        for ref, low in ((basis_v, 0), (snap_v, K)):
            value = ref[:, at]
            high = value.astype(jnp.bfloat16)
            rest = (value - high.astype(jnp.float32)).astype(jnp.bfloat16)
            split_v[low:low + value.shape[0], at] = high
            split_v[K + NEW + low:K + NEW + low + value.shape[0], at] = rest
        both = split_v[:, at]
        term = lax.dot_general(both, both, (((1,), (1,)), ((), ())), preferred_element_type=jnp.float32)
        full = term if full is None else full + term
    half = K + NEW
    return (full[:half, :half] + full[half:, half:]) + (full[half:, :half] + full[:half, half:])


def gram_kernel(na, ny, nz, basis_hbm, snap_hbm, total_ref, split_hbm,
                basis_v, snap_v, split_v, packed, partner, chip, s1a, s1b, s2a, s2b, mids, gathered,
                load_sems, store_sem, send_sems, recv_sems):
    x, y, z = lax.axis_index("gx"), lax.axis_index("gy"), lax.axis_index("gz")
    deep = na // 2
    level, core = x // 2, lax.rem(x, 2)
    cols = basis_v.shape[1]
    loads = []
    for i in range(cols // CHUNK):
        at = pl.ds(i * CHUNK, CHUNK)
        loads.append((
            pltpu.make_async_copy(basis_hbm.at[:, at], basis_v.at[:, at], load_sems.at[0, i]),
            pltpu.make_async_copy(snap_hbm.at[:, at], snap_v.at[:, at], load_sems.at[1, i]),
        ))
        for copy in loads[-1]:
            copy.start()

    def hops(d, n):
        return min(d, n - d)

    other = {"gx": x + 1 - 2 * core}
    plane = [(hops(dy, ny) + hops(dz, nz), {"gy": lax.rem(y + dy, ny), "gz": lax.rem(z + dz, nz)})
             for dy in range(ny) for dz in range(nz) if dy or dz]
    line = [(hops(d, deep), {"gx": lax.rem(level + d, deep) * 2 + core}) for d in range(1, deep)]
    barrier = pltpu.get_barrier_semaphore()
    for device in [other] + [d for _, d in plane + line]:
        pl.semaphore_signal(barrier, inc=1, device_id=device, device_id_type=MESH)

    gram = split_gram(loads, basis_v, snap_v, split_v)
    store = pltpu.make_async_copy(split_v, split_hbm, store_sem)
    store.start()
    half = K + NEW
    gap = jnp.zeros((K, 128 - half), jnp.float32)
    upper = jnp.concatenate([gram[:K], gap], axis=1)
    lower = jnp.concatenate([gram[K:2 * K, K:], gram[2 * K:, K:]], axis=1)
    rows = K // 2
    for i in range(2):
        packed[0, i] = upper[i * rows:(i + 1) * rows]
        packed[1, i] = lower[i * rows:(i + 1) * rows]

    pl.semaphore_wait(barrier, 1 + len(plane) + len(line))

    def send(phase, source, target, device):
        pltpu.make_async_remote_copy(
            src_ref=source, dst_ref=target, send_sem=send_sems.at[phase], recv_sem=recv_sems.at[phase],
            device_id=device, device_id_type=MESH).start()

    def arrive(phase, ref):
        pltpu.make_async_copy(ref, ref, recv_sems.at[phase]).wait()

    def sent(phase, ref):
        pltpu.make_async_copy(ref, ref, send_sems.at[phase]).wait()

    here = y * nz + z
    some_plane, some_line = pl.ds(0, len(plane)), pl.ds(0, len(line))
    send(0, packed.at[1 - core], partner, other)
    arrive(0, partner)
    for i in range(2):
        chip[i] = packed[core, i] + partner[i]
    for far, which, device in sorted(
            [(far, 0, device) for far, device in plane] + [(far, 1, device) for far, device in line],
            key=lambda entry: -entry[0]):
        if which == 0:
            send(1, chip.at[0], s1a.at[here], device)
        else:
            send(2, chip.at[1], s1b.at[level], device)
    s1a[here] = chip[0]
    s1b[level] = chip[1]
    arrive(2, s1b.at[some_line])
    mids[1] = tree_sum([s1b[i] for i in range(deep)])
    for far, device in sorted(plane, key=lambda entry: -entry[0]):
        send(3, mids.at[1], s2b.at[here], device)
    s2b[here] = mids[1]
    arrive(1, s1a.at[some_plane])
    mids[0] = tree_sum([s1a[i] for i in range(ny * nz)])
    for far, device in sorted(line, key=lambda entry: -entry[0]):
        send(4, mids.at[0], s2a.at[level], device)
    s2a[level] = mids[0]
    arrive(4, s2a.at[some_line])
    gathered[core, 0] = tree_sum([s2a[i] for i in range(deep)])
    arrive(3, s2b.at[some_plane])
    gathered[core, 1] = tree_sum([s2b[i] for i in range(ny * nz)])
    send(5, gathered.at[core], gathered.at[core], other)
    arrive(5, gathered.at[1 - core])
    total_ref[...] = gathered[...]
    sent(0, partner)
    sent(1, s1a.at[some_plane])
    sent(2, s1b.at[some_line])
    sent(3, s2b.at[some_plane])
    sent(4, s2a.at[some_line])
    sent(5, partner)
    store.wait()


def update_kernel(rows, total_ref, sigma_ref, split_hbm, modes_hbm, values_ref, split_v, modes_v, load_sem, out_sems):
    cols = split_v.shape[1]
    load = pltpu.make_async_copy(split_hbm, split_v, load_sem)
    load.start()
    total = total_ref[...] * (1.0 / rows)
    upper, lower = total[:K], total[K:]
    gss = jnp.concatenate([lower[:, :NEW], lower[:, NEW:]], axis=0)
    coef, values = dense(upper[:, :K], upper[:, K:K + NEW], gss, sigma_ref[...])
    eye = lax.broadcasted_iota(jnp.int32, (K, K), 0) == lax.broadcasted_iota(jnp.int32, (K, K), 1)
    values_ref[...] = jnp.sum(jnp.where(eye, values, 0.0), axis=0, keepdims=True)
    coef = coef[:, :K + NEW]
    high = coef.astype(jnp.bfloat16).astype(jnp.float32)
    rest = coef - high
    left = jnp.concatenate([
        jnp.concatenate([high, high], axis=1), jnp.concatenate([rest, rest], axis=1)], axis=0).astype(jnp.bfloat16)
    load.wait()
    copies = []
    for i in range(cols // CHUNK):
        at = slice(i * CHUNK, (i + 1) * CHUNK)
        both = jnp.dot(left, split_v[:, at], preferred_element_type=jnp.float32)
        modes_v[:, at] = both[:K] + both[K:]
        span = pl.ds(i * CHUNK, CHUNK)
        copies.append(pltpu.make_async_copy(modes_v.at[:, span], modes_hbm.at[:, span], out_sems.at[i]))
        copies[-1].start()
    for copy in copies:
        copy.wait()


def per_device(basis, sigma, snapshots):
    na, ny, nz = (lax.axis_size(a) for a in AXES)
    cols = basis.shape[1]
    rows = cols * na * ny * nz
    vmem = pl.BlockSpec(memory_space=pltpu.VMEM)
    hbm = pl.BlockSpec(memory_space=pltpu.HBM)
    quarter = (K // 2, 128)
    def slots(*count):
        return pltpu.VMEM(count + quarter, jnp.float32)
    total, split = pl.pallas_call(
        functools.partial(gram_kernel, na, ny, nz),
        out_shape=(jax.ShapeDtypeStruct((2, 2) + quarter, jnp.float32),
                   jax.ShapeDtypeStruct((STACK, cols), jnp.bfloat16)),
        in_specs=[hbm, hbm],
        out_specs=(vmem, hbm),
        scratch_shapes=[
            pltpu.VMEM((K, cols), jnp.float32),
            pltpu.VMEM((NEW, cols), jnp.float32),
            pltpu.VMEM((STACK, cols), jnp.bfloat16),
            slots(2, 2), slots(2), slots(2),
            slots(ny * nz), slots(na // 2), slots(na // 2), slots(ny * nz), slots(2), slots(2, 2),
            pltpu.SemaphoreType.DMA((2, cols // CHUNK)),
            pltpu.SemaphoreType.DMA,
            pltpu.SemaphoreType.DMA((6,)),
            pltpu.SemaphoreType.DMA((6,)),
        ],
        compiler_params=pltpu.CompilerParams(
            collective_id=0, has_side_effects=True, vmem_limit_bytes=53 * 1024 * 1024),
        name="gram_reduce",
    )(basis, snapshots)
    modes, values = pl.pallas_call(
        functools.partial(update_kernel, rows),
        out_shape=(jax.ShapeDtypeStruct((K, cols), jnp.float32),
                   jax.ShapeDtypeStruct((1, K), jnp.float32)),
        in_specs=[vmem, vmem, hbm],
        out_specs=(hbm, vmem),
        scratch_shapes=[
            pltpu.VMEM((STACK, cols), jnp.bfloat16), pltpu.VMEM((K, cols), jnp.float32),
            pltpu.SemaphoreType.DMA, pltpu.SemaphoreType.DMA((cols // CHUNK,))],
        compiler_params=pltpu.CompilerParams(vmem_limit_bytes=53 * 1024 * 1024),
        name="modes_update",
    )(total.reshape(2 * K, 128), sigma.reshape(1, K), split)
    return modes, values.reshape(K)


def solution(mesh):
    placed = (P(None, AXES), P(), P(None, AXES))
    return jax.shard_map(
        per_device, mesh=mesh, in_specs=placed, out_specs=(P(None, AXES), P()), check_vma=False)
```

```python
import functools

import jax
import jax.numpy as jnp
from jax import lax
from jax.experimental import pallas as pl
from jax.experimental.pallas import tpu as pltpu
from jax.sharding import PartitionSpec as P

AXES = ("gx", "gy", "gz")
MESH = pl.DeviceIdType.MESH
HIGH = lax.Precision.HIGHEST
K, NEW = 32, 64

def dot(a, b): return jnp.dot(a, b, precision=HIGH, preferred_element_type=jnp.float32)
def dot_t(a, b): return lax.dot_general(a, b, (((1,), (1,)), ((), ())), precision=HIGH, preferred_element_type=jnp.float32)

def eliminate(N, U):
    nb = N.shape[0] // 8
    Nb = [N[8*i:8*i+8] for i in range(nb)]
    Ub = [U[8*i:8*i+8] for i in range(nb)]
    row = lax.broadcasted_iota(jnp.int32, (8, 128), 0)
    L = U.shape[1]
    def wide(x, width):
        return x[:, :width] if width <= 128 else jnp.concatenate([x] * (width // 128), axis=1)
    out = []
    for kb in range(nb):
        X = {}
        for j in range(8):
            for i in range(kb, nb):
                X[j, i] = jnp.broadcast_to(Nb[i][:, 8*kb+j:8*kb+j+1], (8, 128))
        scale = jnp.ones((8, 128), jnp.float32)
        for r in range(0, 8, 2):
            spread = lambda x, s: jnp.broadcast_to(x[s:s+1], (8, x.shape[1]))
            a = spread(X[r, kb], r); b = spread(X[r+1, kb], r); c = spread(X[r+1, kb], r+1)
            det = a*c - b*b
            rdet = 1.0 / det
            ra = 1.0 / a
            f1 = {}; f2 = {}
            for i in range(kb, nb):
                f1[i] = (c*X[r, i] - b*X[r+1, i]) * rdet
                f2[i] = (a*X[r+1, i] - b*X[r, i]) * rdet
                if i == kb:
                    f1[i] = jnp.where(row > r+1, f1[i], jnp.where(row == r+1, b*ra, 0.0))
                    f2[i] = jnp.where(row > r+1, f2[i], 0.0)
            for j in range(r+2, 8):
                xa = spread(X[j, kb], r); xb = spread(X[j, kb], r+1)
                for i in range(kb, nb):
                    X[j, i] = X[j, i] - f1[i]*xa - f2[i]*xb
            na = spread(Nb[kb], r); nbb = spread(Nb[kb], r+1)
            ua = spread(Ub[kb], r); ub = spread(Ub[kb], r+1)
            for i in range(kb, nb):
                if kb < nb-1:
                    w = Nb[i].shape[1]
                    Nb[i] = Nb[i] - wide(f1[i], w)*na - wide(f2[i], w)*nbb
                Ub[i] = Ub[i] - wide(f1[i], L)*ua - wide(f2[i], L)*ub
            scale = jnp.where(row == r, lax.rsqrt(a), jnp.where(row == r+1, lax.rsqrt(det*ra), scale))
        out.append(Ub[kb] * wide(scale, L))
    return jnp.concatenate(out, axis=0)

def dense(gbb, f, gss, sigma_row):
    ft = f.T
    t = dot(gbb, f)
    c = 2.0*f - t
    ct = 2.0*ft - dot(ft, gbb)
    h = dot(gbb, c) - f
    gram = gss + dot(jnp.concatenate([ct, -ft], 1), jnp.concatenate([h, c], 0))
    eye = lax.broadcasted_iota(jnp.int32, (K, K), 0) == lax.broadcasted_iota(jnp.int32, (K, K), 1)
    eye2 = lax.broadcasted_iota(jnp.int32, (NEW, NEW), 0) == lax.broadcasted_iota(jnp.int32, (NEW, NEW), 1)
    tau = jnp.sum(c*c, keepdims=True).reshape(1,1) + jnp.sum(jnp.where(eye2, gss, 0.0), keepdims=True).reshape(1,1) + jnp.sum(sigma_row*sigma_row, keepdims=True).reshape(1,1)
    rt = 1.0 / tau
    rs = lax.rsqrt(tau)
    sig2 = jnp.where(eye, sigma_row*sigma_row, 0.0)
    p = (sig2 + dot_t(c, c)) * rt
    cu = c
    c = c*rs; ct = ct*rs; gram = gram*rt
    cg = dot(c, gram); cgt = dot(gram, ct); g2 = dot(gram, gram)
    z32 = jnp.zeros((K, 32), jnp.float32); z64 = jnp.zeros((NEW, 32), jnp.float32)
    top = jnp.concatenate([p, c, z32, p, cg, z32], 1)
    bot = jnp.concatenate([cgt, gram, z64, cgt, g2, z64], 1)
    W = jnp.concatenate([top, bot], 0)
    VZ = top
    for step in range(4):
        V = VZ[:, :96]; Z = VZ[:, 128:224]
        N = dot_t(Z, V)
        VZ = eliminate(N, dot(V, W) if step < 3 else VZ)
    Y = VZ[:, :128]
    P = Y[:, :32]; w = Y[:, 32:96]
    Z = jnp.concatenate([P, dot(w, gram), z32], 1)
    N = dot_t(Z, Y)
    YS = dot(Y[:, :96], W[:, 128:])
    pb = P - dot(w, ct)
    U = jnp.concatenate([pb, w*rs, z32, Y, YS], 1)
    U = eliminate(N, U)
    ritz = jnp.sum(U[:, 128:224] * U[:, 256:352], axis=1, keepdims=True)
    values = jnp.sqrt(ritz * tau)
    return U[:, :128], values


CHUNK = 2048
STACK = 2 * (K + NEW)


def tree_sum(values):
    while len(values) > 1:
        values = [a + b for a, b in zip(values[::2], values[1::2])] + values[len(values) // 2 * 2:]
    return values[0]


def split_gram(loads, basis_v, snap_v, split_v):
    full = None
    for i, pair in enumerate(loads):
        for copy in pair:
            copy.wait()
        at = slice(i * CHUNK, (i + 1) * CHUNK)
        for ref, low in ((basis_v, 0), (snap_v, K)):
            value = ref[:, at]
            high = value.astype(jnp.bfloat16)
            rest = (value - high.astype(jnp.float32)).astype(jnp.bfloat16)
            split_v[low:low + value.shape[0], at] = high
            split_v[K + NEW + low:K + NEW + low + value.shape[0], at] = rest
        both = split_v[:, at]
        term = lax.dot_general(both, both, (((1,), (1,)), ((), ())), preferred_element_type=jnp.float32)
        full = term if full is None else full + term
    half = K + NEW
    return (full[:half, :half] + full[half:, half:]) + (full[half:, :half] + full[:half, half:])


def update_kernel(na, ny, nz, basis_hbm, sigma_ref, snap_hbm, modes_ref, values_ref,
                basis_v, snap_v, split_v, packed, partner, chip, s1a, s1b, s2a, s2b, mids, gathered,
                load_sems, send_sems, recv_sems):
    x, y, z = lax.axis_index("gx"), lax.axis_index("gy"), lax.axis_index("gz")
    deep = na // 2
    level, core = x // 2, lax.rem(x, 2)
    cols = basis_v.shape[1]
    loads = []
    for i in range(cols // CHUNK):
        at = pl.ds(i * CHUNK, CHUNK)
        loads.append((
            pltpu.make_async_copy(basis_hbm.at[:, at], basis_v.at[:, at], load_sems.at[0, i]),
            pltpu.make_async_copy(snap_hbm.at[:, at], snap_v.at[:, at], load_sems.at[1, i]),
        ))
        for copy in loads[-1]:
            copy.start()

    def hops(d, n):
        return min(d, n - d)

    other = {"gx": x + 1 - 2 * core}
    plane = [(hops(dy, ny) + hops(dz, nz), {"gy": lax.rem(y + dy, ny), "gz": lax.rem(z + dz, nz)})
             for dy in range(ny) for dz in range(nz) if dy or dz]
    line = [(hops(d, deep), {"gx": lax.rem(level + d, deep) * 2 + core}) for d in range(1, deep)]
    barrier = pltpu.get_barrier_semaphore()
    for device in [other] + [d for _, d in plane + line]:
        pl.semaphore_signal(barrier, inc=1, device_id=device, device_id_type=MESH)

    gram = split_gram(loads, basis_v, snap_v, split_v)
    half = K + NEW
    gap = jnp.zeros((K, 128 - half), jnp.float32)
    upper = jnp.concatenate([gram[:K], gap], axis=1)
    lower = jnp.concatenate([gram[K:2 * K, K:], gram[2 * K:, K:]], axis=1)
    rows = K // 2
    for i in range(2):
        packed[0, i] = upper[i * rows:(i + 1) * rows]
        packed[1, i] = lower[i * rows:(i + 1) * rows]

    pl.semaphore_wait(barrier, 1 + len(plane) + len(line))

    def send(phase, source, target, device):
        pltpu.make_async_remote_copy(
            src_ref=source, dst_ref=target, send_sem=send_sems.at[phase], recv_sem=recv_sems.at[phase],
            device_id=device, device_id_type=MESH).start()

    def arrive(phase, ref):
        pltpu.make_async_copy(ref, ref, recv_sems.at[phase]).wait()

    def sent(phase, ref):
        pltpu.make_async_copy(ref, ref, send_sems.at[phase]).wait()

    here = y * nz + z
    some_plane, some_line = pl.ds(0, len(plane)), pl.ds(0, len(line))
    send(0, packed.at[1 - core], partner, other)
    arrive(0, partner)
    for i in range(2):
        chip[i] = packed[core, i] + partner[i]
    for far, which, device in sorted(
            [(far, 0, device) for far, device in plane] + [(far, 1, device) for far, device in line],
            key=lambda entry: -entry[0]):
        if which == 0:
            send(1, chip.at[0], s1a.at[here], device)
        else:
            send(2, chip.at[1], s1b.at[level], device)
    s1a[here] = chip[0]
    s1b[level] = chip[1]
    arrive(2, s1b.at[some_line])
    mids[1] = tree_sum([s1b[i] for i in range(deep)])
    for far, device in sorted(plane, key=lambda entry: -entry[0]):
        send(3, mids.at[1], s2b.at[here], device)
    s2b[here] = mids[1]
    arrive(1, s1a.at[some_plane])
    mids[0] = tree_sum([s1a[i] for i in range(ny * nz)])
    for far, device in sorted(line, key=lambda entry: -entry[0]):
        send(4, mids.at[0], s2a.at[level], device)
    s2a[level] = mids[0]
    arrive(4, s2a.at[some_line])
    gathered[core, 0] = tree_sum([s2a[i] for i in range(deep)])
    arrive(3, s2b.at[some_plane])
    gathered[core, 1] = tree_sum([s2b[i] for i in range(ny * nz)])
    send(5, gathered.at[core], gathered.at[core], other)
    arrive(5, gathered.at[1 - core])
    upper = jnp.concatenate([gathered[0, 0], gathered[0, 1]], axis=0) * (1.0 / (cols * na * ny * nz))
    lower = jnp.concatenate([gathered[1, 0], gathered[1, 1]], axis=0) * (1.0 / (cols * na * ny * nz))
    gss = jnp.concatenate([lower[:, :NEW], lower[:, NEW:]], axis=0)
    coef, values = dense(upper[:, :K], upper[:, K:K + NEW], gss, sigma_ref[...])
    eye = lax.broadcasted_iota(jnp.int32, (K, K), 0) == lax.broadcasted_iota(jnp.int32, (K, K), 1)
    values_ref[...] = jnp.sum(jnp.where(eye, values, 0.0), axis=0, keepdims=True)
    coef = coef[:, :K + NEW]
    high = coef.astype(jnp.bfloat16).astype(jnp.float32)
    rest = coef - high
    left = jnp.concatenate([
        jnp.concatenate([high, high], axis=1), jnp.concatenate([rest, rest], axis=1)], axis=0).astype(jnp.bfloat16)
    for i in range(cols // CHUNK):
        at = slice(i * CHUNK, (i + 1) * CHUNK)
        both = jnp.dot(left, split_v[:, at], preferred_element_type=jnp.float32)
        modes_ref[:, at] = both[:K] + both[K:]
    sent(0, partner)
    sent(1, s1a.at[some_plane])
    sent(2, s1b.at[some_line])
    sent(3, s2b.at[some_plane])
    sent(4, s2a.at[some_line])
    sent(5, partner)


def per_device(basis, sigma, snapshots):
    na, ny, nz = (lax.axis_size(a) for a in AXES)
    cols = basis.shape[1]
    vmem = pl.BlockSpec(memory_space=pltpu.VMEM)
    hbm = pl.BlockSpec(memory_space=pltpu.HBM)
    quarter = (K // 2, 128)
    def slots(*count):
        return pltpu.VMEM(count + quarter, jnp.float32)
    modes, values = pl.pallas_call(
        functools.partial(update_kernel, na, ny, nz),
        out_shape=(jax.ShapeDtypeStruct((K, cols), jnp.float32),
                   jax.ShapeDtypeStruct((1, K), jnp.float32)),
        in_specs=[hbm, vmem, hbm],
        out_specs=(vmem, vmem),
        scratch_shapes=[
            pltpu.VMEM((K, cols), jnp.float32),
            pltpu.VMEM((NEW, cols), jnp.float32),
            pltpu.VMEM((STACK, cols), jnp.bfloat16),
            slots(2, 2), slots(2), slots(2),
            slots(ny * nz), slots(na // 2), slots(na // 2), slots(ny * nz), slots(2), slots(2, 2),
            pltpu.SemaphoreType.DMA((2, cols // CHUNK)),
            pltpu.SemaphoreType.DMA((6,)),
            pltpu.SemaphoreType.DMA((6,)),
        ],
        compiler_params=pltpu.CompilerParams(
            collective_id=0, has_side_effects=True, vmem_limit_bytes=52 * 1024 * 1024),
        name="pod_update",
    )(basis, sigma.reshape(1, K), snapshots)
    return modes, values.reshape(K)


def solution(mesh):
    placed = (P(None, AXES), P(), P(None, AXES))
    return jax.shard_map(
        per_device, mesh=mesh, in_specs=placed, out_specs=(P(None, AXES), P()), check_vma=False)
```

```python
import functools

import jax
import jax.numpy as jnp
from jax import lax
from jax.experimental import pallas as pl
from jax.experimental.pallas import tpu as pltpu
from jax.sharding import PartitionSpec as P

AXES = ("gx", "gy", "gz")
MESH = pl.DeviceIdType.MESH
HIGH = lax.Precision.HIGHEST
K, NEW = 32, 64

def dot(a, b): return jnp.dot(a, b, precision=HIGH, preferred_element_type=jnp.float32)
def dot_t(a, b): return lax.dot_general(a, b, (((1,), (1,)), ((), ())), precision=HIGH, preferred_element_type=jnp.float32)

def eliminate(N, U):
    nb = N.shape[0] // 8
    Nb = [N[8*i:8*i+8] for i in range(nb)]
    Ub = [U[8*i:8*i+8] for i in range(nb)]
    row = lax.broadcasted_iota(jnp.int32, (8, 128), 0)
    L = U.shape[1]
    def wide(x, width):
        return x[:, :width] if width <= 128 else jnp.concatenate([x] * (width // 128), axis=1)
    def column_splats(kb, Nb):
        return {(j, i): jnp.broadcast_to(Nb[i][:, 8*kb+j:8*kb+j+1], (8, 128))
                for j in range(8) for i in range(kb, nb)}
    out = []
    for kb in range(nb):
        X = ahead if kb else column_splats(0, Nb)
        ahead = {}
        scale = jnp.ones((8, 128), jnp.float32)
        for r in range(0, 8, 2):
            if r == 2 and kb < nb-1:
                ahead = column_splats(kb+1, Nb)
            spread = lambda x, s: jnp.broadcast_to(x[s:s+1], (8, x.shape[1]))
            a = spread(X[r, kb], r); b = spread(X[r+1, kb], r); c = spread(X[r+1, kb], r+1)
            det = a*c - b*b
            rdet = 1.0 / det
            ra = 1.0 / a
            f1 = {}; f2 = {}
            for i in range(kb, nb):
                f1[i] = (c*X[r, i] - b*X[r+1, i]) * rdet
                f2[i] = (a*X[r+1, i] - b*X[r, i]) * rdet
                if i == kb:
                    f1[i] = jnp.where(row > r+1, f1[i], jnp.where(row == r+1, b*ra, 0.0))
                    f2[i] = jnp.where(row > r+1, f2[i], 0.0)
            for j in range(r+2, 8):
                xa = spread(X[j, kb], r); xb = spread(X[j, kb], r+1)
                for i in range(kb, nb):
                    X[j, i] = X[j, i] - f1[i]*xa - f2[i]*xb
            for j in range(8 if ahead else 0):
                xa = spread(X[r, kb+1], j); xb = spread(X[r+1, kb+1], j)
                for i in range(kb+1, nb):
                    ahead[j, i] = ahead[j, i] - f1[i]*xa - f2[i]*xb
            na = spread(Nb[kb], r); nbb = spread(Nb[kb], r+1)
            ua = spread(Ub[kb], r); ub = spread(Ub[kb], r+1)
            for i in range(kb, nb):
                if kb < nb-1:
                    w = Nb[i].shape[1]
                    Nb[i] = Nb[i] - wide(f1[i], w)*na - wide(f2[i], w)*nbb
                Ub[i] = Ub[i] - wide(f1[i], L)*ua - wide(f2[i], L)*ub
            scale = jnp.where(row == r, lax.rsqrt(a), jnp.where(row == r+1, lax.rsqrt(det*ra), scale))
        out.append(Ub[kb] * wide(scale, L))
    return jnp.concatenate(out, axis=0)

def dense(gbb, f, gss, sigma_row):
    ft = f.T
    t = dot(gbb, f)
    c = 2.0*f - t
    ct = 2.0*ft - dot(ft, gbb)
    h = dot(gbb, c) - f
    gram = gss + dot(jnp.concatenate([ct, -ft], 1), jnp.concatenate([h, c], 0))
    eye = lax.broadcasted_iota(jnp.int32, (K, K), 0) == lax.broadcasted_iota(jnp.int32, (K, K), 1)
    eye2 = lax.broadcasted_iota(jnp.int32, (NEW, NEW), 0) == lax.broadcasted_iota(jnp.int32, (NEW, NEW), 1)
    tau = jnp.sum(c*c, keepdims=True).reshape(1,1) + jnp.sum(jnp.where(eye2, gss, 0.0), keepdims=True).reshape(1,1) + jnp.sum(sigma_row*sigma_row, keepdims=True).reshape(1,1)
    rt = 1.0 / tau
    rs = lax.rsqrt(tau)
    sig2 = jnp.where(eye, sigma_row*sigma_row, 0.0)
    p = (sig2 + dot_t(c, c)) * rt
    cu = c
    c = c*rs; ct = ct*rs; gram = gram*rt
    cg = dot(c, gram); cgt = dot(gram, ct); g2 = dot(gram, gram)
    z32 = jnp.zeros((K, 32), jnp.float32); z64 = jnp.zeros((NEW, 32), jnp.float32)
    top = jnp.concatenate([p, c, z32, p, cg, z32], 1)
    bot = jnp.concatenate([cgt, gram, z64, cgt, g2, z64], 1)
    W = jnp.concatenate([top, bot], 0)
    VZ = top
    for step in range(4):
        V = VZ[:, :96]; Z = VZ[:, 128:224]
        N = dot_t(Z, V)
        VZ = eliminate(N, dot(V, W) if step < 3 else VZ)
    Y = VZ[:, :128]
    P = Y[:, :32]; w = Y[:, 32:96]
    Z = jnp.concatenate([P, dot(w, gram), z32], 1)
    N = dot_t(Z, Y)
    YS = dot(Y[:, :96], W[:, 128:])
    pb = P - dot(w, ct)
    U = jnp.concatenate([pb, w*rs, z32, Y, YS], 1)
    U = eliminate(N, U)
    ritz = jnp.sum(U[:, 128:224] * U[:, 256:352], axis=1, keepdims=True)
    values = jnp.sqrt(ritz * tau)
    return U[:, :128], values


CHUNK = 2048
LOAD = 2048
PARTS = 4
STACK = 2 * (K + NEW)


def tree_sum(values):
    while len(values) > 1:
        values = [a + b for a, b in zip(values[::2], values[1::2])] + values[len(values) // 2 * 2:]
    return values[0]


def split_gram(loads, basis_v, snap_v, split_v):
    full = None
    for i, pair in enumerate(loads):
        for copy in pair:
            copy.wait()
        at = slice(i * LOAD, (i + 1) * LOAD)
        for ref, low in ((basis_v, 0), (snap_v, K)):
            value = ref[:, at]
            high = value.astype(jnp.bfloat16)
            rest = (value - high.astype(jnp.float32)).astype(jnp.bfloat16)
            split_v[low:low + value.shape[0], at] = high
            split_v[K + NEW + low:K + NEW + low + value.shape[0], at] = rest
        both = split_v[:, at]
        term = lax.dot_general(both, both, (((1,), (1,)), ((), ())), preferred_element_type=jnp.float32)
        full = term if full is None else full + term
    half = K + NEW
    return (full[:half, :half] + full[half:, half:]) + (full[half:, :half] + full[:half, half:])


def update_kernel(na, ny, nz, basis_hbm, sigma_hbm, snap_hbm, modes_ref, values_ref,
                basis_v, snap_v, split_v, packed, partner, chip, s1a, s1b, s2a, s2b, mids, gathered,
                sigma_ref, sigma_sem, load_sems, send_sems, recv_sems):
    x, y, z = lax.axis_index("gx"), lax.axis_index("gy"), lax.axis_index("gz")
    deep = na // 2
    level, core = x // 2, lax.rem(x, 2)
    cols = basis_v.shape[1]
    loads = []
    for i in range(cols // LOAD):
        at = pl.ds(i * LOAD, LOAD)
        loads.append((
            pltpu.make_async_copy(basis_hbm.at[:, at], basis_v.at[:, at], load_sems.at[0, i]),
            pltpu.make_async_copy(snap_hbm.at[:, at], snap_v.at[:, at], load_sems.at[1, i]),
        ))
        for copy in loads[-1]:
            copy.start()

    sigma_load = pltpu.make_async_copy(sigma_hbm, sigma_ref, sigma_sem)
    sigma_load.start()

    def hops(d, n):
        return min(d, n - d)

    other = {"gx": x + 1 - 2 * core}
    plane = [(hops(dy, ny) + hops(dz, nz), {"gy": lax.rem(y + dy, ny), "gz": lax.rem(z + dz, nz)})
             for dy in range(ny) for dz in range(nz) if dy or dz]
    line = [(hops(d, deep), {"gx": lax.rem(level + d, deep) * 2 + core}) for d in range(1, deep)]
    barrier = pltpu.get_barrier_semaphore()
    for device in [other] + [d for _, d in plane + line]:
        pl.semaphore_signal(barrier, inc=1, device_id=device, device_id_type=MESH)

    gram = split_gram(loads, basis_v, snap_v, split_v)
    half = K + NEW
    gap = jnp.zeros((K, 128 - half), jnp.float32)
    upper = jnp.concatenate([gram[:K], gap], axis=1)
    lower = jnp.concatenate([gram[K:2 * K, K:], gram[2 * K:, K:]], axis=1)
    rows = K // 2
    for i in range(2):
        packed[0, i] = upper[i * rows:(i + 1) * rows]
        packed[1, i] = lower[i * rows:(i + 1) * rows]

    pl.semaphore_wait(barrier, 1 + len(plane) + len(line))

    def send(phase, source, target, device):
        pltpu.make_async_remote_copy(
            src_ref=source, dst_ref=target, send_sem=send_sems.at[phase], recv_sem=recv_sems.at[phase],
            device_id=device, device_id_type=MESH).start()

    def arrive(phase, ref):
        pltpu.make_async_copy(ref, ref, recv_sems.at[phase]).wait()

    def sent(phase, ref):
        pltpu.make_async_copy(ref, ref, send_sems.at[phase]).wait()

    here = y * nz + z
    some_plane, some_line = pl.ds(0, len(plane)), pl.ds(0, len(line))
    send(0, packed.at[1 - core], partner, other)
    arrive(0, partner)
    for i in range(2):
        chip[i] = packed[core, i] + partner[i]
    for far, which, device in sorted(
            [(far, 0, device) for far, device in plane] + [(far, 1, device) for far, device in line],
            key=lambda entry: -entry[0]):
        if which == 0:
            send(1, chip.at[0], s1a.at[here], device)
        else:
            send(2, chip.at[1], s1b.at[level], device)
    s1a[here] = chip[0]
    s1b[level] = chip[1]
    arrive(2, s1b.at[some_line])
    mids[1] = tree_sum([s1b[i] for i in range(deep)])
    for far, device in sorted(plane, key=lambda entry: -entry[0]):
        send(3, mids.at[1], s2b.at[here], device)
    s2b[here] = mids[1]
    arrive(1, s1a.at[some_plane])
    mids[0] = tree_sum([s1a[i] for i in range(ny * nz)])
    for far, device in sorted(line, key=lambda entry: -entry[0]):
        send(4, mids.at[0], s2a.at[level], device)
    s2a[level] = mids[0]
    arrive(4, s2a.at[some_line])
    gathered[core, 0] = tree_sum([s2a[i] for i in range(deep)])
    arrive(3, s2b.at[some_plane])
    gathered[core, 1] = tree_sum([s2b[i] for i in range(ny * nz)])
    send(5, gathered.at[core], gathered.at[core], other)
    arrive(5, gathered.at[1 - core])
    sigma_load.wait()
    upper = jnp.concatenate([gathered[0, 0], gathered[0, 1]], axis=0) * (1.0 / (cols * na * ny * nz))
    lower = jnp.concatenate([gathered[1, 0], gathered[1, 1]], axis=0) * (1.0 / (cols * na * ny * nz))
    gss = jnp.concatenate([lower[:, :NEW], lower[:, NEW:]], axis=0)
    coef, values = dense(upper[:, :K], upper[:, K:K + NEW], gss, sigma_ref[...])
    eye = lax.broadcasted_iota(jnp.int32, (K, K), 0) == lax.broadcasted_iota(jnp.int32, (K, K), 1)
    values_ref[...] = jnp.sum(jnp.where(eye, values, 0.0), axis=0, keepdims=True)
    coef = coef[:, :K + NEW]
    high = coef.astype(jnp.bfloat16).astype(jnp.float32)
    rest = coef - high
    left = jnp.concatenate([
        jnp.concatenate([high, high], axis=1), jnp.concatenate([rest, rest], axis=1)], axis=0).astype(jnp.bfloat16)
    for i in range(cols // CHUNK):
        at = slice(i * CHUNK, (i + 1) * CHUNK)
        both = jnp.dot(left, split_v[:, at], preferred_element_type=jnp.float32)
        modes_ref[:, at] = both[:K] + both[K:]
    sent(0, partner)
    sent(1, s1a.at[some_plane])
    sent(2, s1b.at[some_line])
    sent(3, s2b.at[some_plane])
    sent(4, s2a.at[some_line])
    sent(5, partner)


def finish_kernel(modes_ref, values_ref, modes_hbm, values_hbm, sems):
    cols = modes_hbm.shape[1]
    parts = sems.shape[0] - 1
    copies = [pltpu.make_async_copy(values_ref, values_hbm, sems.at[parts])]
    copies[0].start()
    for i in range(parts):
        at = pl.ds(i * (cols // parts), cols // parts)
        copies.append(pltpu.make_async_copy(modes_ref.at[:, at], modes_hbm.at[:, at], sems.at[i]))
        copies[-1].start()
    for copy in copies:
        copy.wait()


def per_device(basis, sigma, snapshots):
    na, ny, nz = (lax.axis_size(a) for a in AXES)
    cols = basis.shape[1]
    vmem = pl.BlockSpec(memory_space=pltpu.VMEM)
    hbm = pl.BlockSpec(memory_space=pltpu.HBM)
    quarter = (K // 2, 128)
    def slots(*count):
        return pltpu.VMEM(count + quarter, jnp.float32)
    modes, values = pl.pallas_call(
        functools.partial(update_kernel, na, ny, nz),
        out_shape=(jax.ShapeDtypeStruct((K, cols), jnp.float32),
                   jax.ShapeDtypeStruct((1, K), jnp.float32)),
        in_specs=[hbm, hbm, hbm],
        out_specs=(vmem, vmem),
        scratch_shapes=[
            pltpu.VMEM((K, cols), jnp.float32),
            pltpu.VMEM((NEW, cols), jnp.float32),
            pltpu.VMEM((STACK, cols), jnp.bfloat16),
            slots(2, 2), slots(2), slots(2),
            slots(ny * nz), slots(na // 2), slots(na // 2), slots(ny * nz), slots(2), slots(2, 2),
            pltpu.VMEM((1, K), jnp.float32),
            pltpu.SemaphoreType.DMA,
            pltpu.SemaphoreType.DMA((2, cols // LOAD)),
            pltpu.SemaphoreType.DMA((6,)),
            pltpu.SemaphoreType.DMA((6,)),
        ],
        compiler_params=pltpu.CompilerParams(
            collective_id=0, has_side_effects=True, vmem_limit_bytes=52 * 1024 * 1024),
        name="pod_update",
    )(basis, sigma.reshape(1, K), snapshots)
    modes, values = pl.pallas_call(
        finish_kernel,
        out_shape=(jax.ShapeDtypeStruct((K, cols), jnp.float32),
                   jax.ShapeDtypeStruct((1, K), jnp.float32)),
        in_specs=[pl.BlockSpec(memory_space=pl.ANY), vmem],
        out_specs=(hbm, hbm),
        scratch_shapes=[pltpu.SemaphoreType.DMA((PARTS + 1,))],
        compiler_params=pltpu.CompilerParams(vmem_limit_bytes=1024 * 1024),
        name="write_out",
    )(modes, values)
    return modes, values.reshape(K)


def solution(mesh):
    placed = (P(None, AXES), P(), P(None, AXES))
    return jax.shard_map(
        per_device, mesh=mesh, in_specs=placed, out_specs=(P(None, AXES), P()), check_vma=False)
```

```python
import functools

import jax
import jax.numpy as jnp
from jax import lax
from jax.experimental import pallas as pl
from jax.experimental.pallas import tpu as pltpu
from jax.sharding import PartitionSpec as P

AXES = ("gx", "gy", "gz")
MESH = pl.DeviceIdType.MESH
HIGH = lax.Precision.HIGHEST
K, NEW = 32, 64

def dot(a, b): return jnp.dot(a, b, precision=HIGH, preferred_element_type=jnp.float32)
def dot_t(a, b): return lax.dot_general(a, b, (((1,), (1,)), ((), ())), precision=HIGH, preferred_element_type=jnp.float32)

def eliminate(N, U):
    nb = N.shape[0] // 8
    Nb = [N[8*i:8*i+8] for i in range(nb)]
    Ub = [U[8*i:8*i+8] for i in range(nb)]
    row = lax.broadcasted_iota(jnp.int32, (8, 128), 0)
    L = U.shape[1]
    def wide(x, width):
        return x[:, :width] if width <= 128 else jnp.concatenate([x] * (width // 128), axis=1)
    def column_splats(kb, Nb):
        return {(j, i): jnp.broadcast_to(Nb[i][:, 8*kb+j:8*kb+j+1], (8, 128))
                for j in range(8) for i in range(kb, nb)}
    out = []
    for kb in range(nb):
        X = ahead if kb else column_splats(0, Nb)
        ahead = {}
        scale = jnp.ones((8, 128), jnp.float32)
        for r in range(0, 8, 2):
            if r == 2 and kb < nb-1:
                ahead = column_splats(kb+1, Nb)
            spread = lambda x, s: jnp.broadcast_to(x[s:s+1], (8, x.shape[1]))
            a = spread(X[r, kb], r); b = spread(X[r+1, kb], r); c = spread(X[r+1, kb], r+1)
            det = a*c - b*b
            rdet = 1.0 / det
            ra = 1.0 / a
            f1 = {}; f2 = {}
            for i in range(kb, nb):
                f1[i] = (c*X[r, i] - b*X[r+1, i]) * rdet
                f2[i] = (a*X[r+1, i] - b*X[r, i]) * rdet
                if i == kb:
                    f1[i] = jnp.where(row > r+1, f1[i], jnp.where(row == r+1, b*ra, 0.0))
                    f2[i] = jnp.where(row > r+1, f2[i], 0.0)
            for j in range(r+2, 8):
                xa = spread(X[j, kb], r); xb = spread(X[j, kb], r+1)
                for i in range(kb, nb):
                    X[j, i] = X[j, i] - f1[i]*xa - f2[i]*xb
            for j in range(8 if ahead else 0):
                xa = spread(X[r, kb+1], j); xb = spread(X[r+1, kb+1], j)
                for i in range(kb+1, nb):
                    ahead[j, i] = ahead[j, i] - f1[i]*xa - f2[i]*xb
            na = spread(Nb[kb], r); nbb = spread(Nb[kb], r+1)
            ua = spread(Ub[kb], r); ub = spread(Ub[kb], r+1)
            for i in range(kb, nb):
                if kb < nb-1:
                    w = Nb[i].shape[1]
                    Nb[i] = Nb[i] - wide(f1[i], w)*na - wide(f2[i], w)*nbb
                Ub[i] = Ub[i] - wide(f1[i], L)*ua - wide(f2[i], L)*ub
            scale = jnp.where(row == r, lax.rsqrt(a), jnp.where(row == r+1, lax.rsqrt(det*ra), scale))
        out.append(Ub[kb] * wide(scale, L))
    return jnp.concatenate(out, axis=0)

def project(gbb, f):
    ft = f.T
    t = dot(gbb, f)
    c = 2.0*f - t
    ct = 2.0*ft - dot(ft, gbb)
    return ft, c, ct, dot(gbb, c) - f


def dense(ft, c, ct, h, gss, sigma_row):
    gram = gss + dot(jnp.concatenate([ct, -ft], 1), jnp.concatenate([h, c], 0))
    eye = lax.broadcasted_iota(jnp.int32, (K, K), 0) == lax.broadcasted_iota(jnp.int32, (K, K), 1)
    eye2 = lax.broadcasted_iota(jnp.int32, (NEW, NEW), 0) == lax.broadcasted_iota(jnp.int32, (NEW, NEW), 1)
    tau = jnp.sum(c*c, keepdims=True).reshape(1,1) + jnp.sum(jnp.where(eye2, gss, 0.0), keepdims=True).reshape(1,1) + jnp.sum(sigma_row*sigma_row, keepdims=True).reshape(1,1)
    rt = 1.0 / tau
    rs = lax.rsqrt(tau)
    sig2 = jnp.where(eye, sigma_row*sigma_row, 0.0)
    p = (sig2 + dot_t(c, c)) * rt
    cu = c
    c = c*rs; ct = ct*rs; gram = gram*rt
    cg = dot(c, gram); cgt = dot(gram, ct); g2 = dot(gram, gram)
    z32 = jnp.zeros((K, 32), jnp.float32); z64 = jnp.zeros((NEW, 32), jnp.float32)
    top = jnp.concatenate([p, c, z32, p, cg, z32], 1)
    bot = jnp.concatenate([cgt, gram, z64, cgt, g2, z64], 1)
    W = jnp.concatenate([top, bot], 0)
    VZ = top
    for step in range(4):
        V = VZ[:, :96]; Z = VZ[:, 128:224]
        N = dot_t(Z, V)
        VZ = eliminate(N, dot(V, W) if step < 3 else VZ)
    Y = VZ[:, :128]
    P = Y[:, :32]; w = Y[:, 32:96]
    Z = jnp.concatenate([P, dot(w, gram), z32], 1)
    N = dot_t(Z, Y)
    YS = dot(Y[:, :96], W[:, 128:])
    pb = P - dot(w, ct)
    U = jnp.concatenate([pb, w*rs, z32, Y, YS], 1)
    U = eliminate(N, U)
    ritz = jnp.sum(U[:, 128:224] * U[:, 256:352], axis=1, keepdims=True)
    values = jnp.sqrt(ritz * tau)
    return U[:, :128], values


CHUNK = 2048
LOAD = 2048
PARTS = 4
STACK = 2 * (K + NEW)


def tree_sum(values):
    while len(values) > 1:
        values = [a + b for a, b in zip(values[::2], values[1::2])] + values[len(values) // 2 * 2:]
    return values[0]


def split_gram(loads, basis_v, snap_v, split_v):
    full = None
    for i, pair in enumerate(loads):
        for copy in pair:
            copy.wait()
        at = slice(i * LOAD, (i + 1) * LOAD)
        for ref, low in ((basis_v, 0), (snap_v, K)):
            value = ref[:, at]
            high = value.astype(jnp.bfloat16)
            rest = (value - high.astype(jnp.float32)).astype(jnp.bfloat16)
            split_v[low:low + value.shape[0], at] = high
            split_v[K + NEW + low:K + NEW + low + value.shape[0], at] = rest
        both = split_v[:, at]
        term = lax.dot_general(both, both, (((1,), (1,)), ((), ())), preferred_element_type=jnp.float32)
        full = term if full is None else full + term
    half = K + NEW
    return (full[:half, :half] + full[half:, half:]) + (full[half:, :half] + full[:half, half:])


def update_kernel(na, ny, nz, basis_hbm, sigma_hbm, snap_hbm, modes_ref, values_ref,
                basis_v, snap_v, split_v, packed, partner, chip, s1a, s1b, s2a, s2b, mids, gathered,
                sigma_ref, sigma_sem, load_sems, send_sems, recv_sems):
    x, y, z = lax.axis_index("gx"), lax.axis_index("gy"), lax.axis_index("gz")
    deep = na // 2
    level, core = x // 2, lax.rem(x, 2)
    own = 1 - core
    cols = basis_v.shape[1]
    loads = []
    for i in range(cols // LOAD):
        at = pl.ds(i * LOAD, LOAD)
        loads.append((
            pltpu.make_async_copy(basis_hbm.at[:, at], basis_v.at[:, at], load_sems.at[0, i]),
            pltpu.make_async_copy(snap_hbm.at[:, at], snap_v.at[:, at], load_sems.at[1, i]),
        ))
        for copy in loads[-1]:
            copy.start()

    sigma_load = pltpu.make_async_copy(sigma_hbm, sigma_ref, sigma_sem)
    sigma_load.start()

    here = y * nz + z

    def others_of(me, n):
        return [k + (k - me + n) // n for k in range(n - 1)]

    other = {"gx": x + 1 - 2 * core}
    plane = [{"gy": t // nz, "gz": lax.rem(t, nz)} for t in others_of(here, ny * nz)]
    line = [{"gx": 2 * t + core} for t in others_of(level, deep)]
    barrier = pltpu.get_barrier_semaphore()
    for device in [other] + plane + line:
        pl.semaphore_signal(barrier, inc=1, device_id=device, device_id_type=MESH)

    gram = split_gram(loads, basis_v, snap_v, split_v)
    half = K + NEW
    gap = jnp.zeros((K, 128 - half), jnp.float32)
    upper = jnp.concatenate([gram[:K], gap], axis=1)
    lower = jnp.concatenate([gram[K:2 * K, K:], gram[2 * K:, K:]], axis=1)
    rows = K // 2
    for i in range(2):
        packed[0, i] = upper[i * rows:(i + 1) * rows]
        packed[1, i] = lower[i * rows:(i + 1) * rows]

    pl.semaphore_wait(barrier, 1 + len(plane) + len(line))

    def send(phase, source, target, device):
        pltpu.make_async_remote_copy(
            src_ref=source, dst_ref=target, send_sem=send_sems.at[phase], recv_sem=recv_sems.at[phase],
            device_id=device, device_id_type=MESH).start()

    def arrive(phase, ref):
        pltpu.make_async_copy(ref, ref, recv_sems.at[phase]).wait()

    def sent(phase, ref):
        pltpu.make_async_copy(ref, ref, send_sems.at[phase]).wait()

    some_plane, some_line = pl.ds(0, len(plane)), pl.ds(0, len(line))
    send(0, packed.at[1 - own], partner, other)
    arrive(0, partner)
    for i in range(2):
        chip[i] = packed[own, i] + partner[i]
    order = [(k / len(plane), 0, k) for k in range(len(plane))] + [(k / len(line), 1, k) for k in range(len(line))]
    for _, which, k in sorted(order):
        if which == 0:
            send(1, chip.at[0], s1a.at[here], plane[k])
        else:
            send(2, chip.at[1], s1b.at[level], line[k])
    s1a[here] = chip[0]
    s1b[level] = chip[1]
    arrive(2, s1b.at[some_line])
    mids[1] = tree_sum([s1b[i] for i in range(deep)])
    for device in plane:
        send(3, mids.at[1], s2b.at[here], device)
    s2b[here] = mids[1]
    arrive(1, s1a.at[some_plane])
    mids[0] = tree_sum([s1a[i] for i in range(ny * nz)])
    for device in line:
        send(4, mids.at[0], s2a.at[level], device)
    s2a[level] = mids[0]
    arrive(4, s2a.at[some_line])
    gathered[own, 0] = tree_sum([s2a[i] for i in range(deep)])
    arrive(3, s2b.at[some_plane])
    gathered[own, 1] = tree_sum([s2b[i] for i in range(ny * nz)])
    send(5, gathered.at[own], gathered.at[own], other)
    scale = 1.0 / (cols * na * ny * nz)

    @pl.when(core == 0)
    def _():
        arrive(5, gathered.at[0])

    upper = jnp.concatenate([gathered[0, 0], gathered[0, 1]], axis=0) * scale
    projected = project(upper[:, :K], upper[:, K:K + NEW])

    @pl.when(core == 1)
    def _():
        arrive(5, gathered.at[1])

    sigma_load.wait()
    lower = jnp.concatenate([gathered[1, 0], gathered[1, 1]], axis=0) * scale
    gss = jnp.concatenate([lower[:, :NEW], lower[:, NEW:]], axis=0)
    coef, values = dense(*projected, gss, sigma_ref[...])
    eye = lax.broadcasted_iota(jnp.int32, (K, K), 0) == lax.broadcasted_iota(jnp.int32, (K, K), 1)
    values_ref[...] = jnp.sum(jnp.where(eye, values, 0.0), axis=0, keepdims=True)
    coef = coef[:, :K + NEW]
    high = coef.astype(jnp.bfloat16).astype(jnp.float32)
    rest = coef - high
    left = jnp.concatenate([
        jnp.concatenate([high, high], axis=1), jnp.concatenate([rest, rest], axis=1)], axis=0).astype(jnp.bfloat16)
    for i in range(cols // CHUNK):
        at = slice(i * CHUNK, (i + 1) * CHUNK)
        both = jnp.dot(left, split_v[:, at], preferred_element_type=jnp.float32)
        modes_ref[:, at] = both[:K] + both[K:]
    sent(0, partner)
    sent(1, s1a.at[some_plane])
    sent(2, s1b.at[some_line])
    sent(3, s2b.at[some_plane])
    sent(4, s2a.at[some_line])
    sent(5, partner)


def finish_kernel(modes_ref, values_ref, modes_hbm, values_hbm, sems):
    cols = modes_hbm.shape[1]
    parts = sems.shape[0] - 1
    copies = [pltpu.make_async_copy(values_ref, values_hbm, sems.at[parts])]
    copies[0].start()
    for i in range(parts):
        at = pl.ds(i * (cols // parts), cols // parts)
        copies.append(pltpu.make_async_copy(modes_ref.at[:, at], modes_hbm.at[:, at], sems.at[i]))
        copies[-1].start()
    for copy in copies:
        copy.wait()


def per_device(basis, sigma, snapshots):
    na, ny, nz = (lax.axis_size(a) for a in AXES)
    cols = basis.shape[1]
    vmem = pl.BlockSpec(memory_space=pltpu.VMEM)
    hbm = pl.BlockSpec(memory_space=pltpu.HBM)
    quarter = (K // 2, 128)
    def slots(*count):
        return pltpu.VMEM(count + quarter, jnp.float32)
    modes, values = pl.pallas_call(
        functools.partial(update_kernel, na, ny, nz),
        out_shape=(jax.ShapeDtypeStruct((K, cols), jnp.float32),
                   jax.ShapeDtypeStruct((1, K), jnp.float32)),
        in_specs=[hbm, hbm, hbm],
        out_specs=(vmem, vmem),
        scratch_shapes=[
            pltpu.VMEM((K, cols), jnp.float32),
            pltpu.VMEM((NEW, cols), jnp.float32),
            pltpu.VMEM((STACK, cols), jnp.bfloat16),
            slots(2, 2), slots(2), slots(2),
            slots(ny * nz), slots(na // 2), slots(na // 2), slots(ny * nz), slots(2), slots(2, 2),
            pltpu.VMEM((1, K), jnp.float32),
            pltpu.SemaphoreType.DMA,
            pltpu.SemaphoreType.DMA((2, cols // LOAD)),
            pltpu.SemaphoreType.DMA((6,)),
            pltpu.SemaphoreType.DMA((6,)),
        ],
        compiler_params=pltpu.CompilerParams(
            collective_id=0, has_side_effects=True, vmem_limit_bytes=52 * 1024 * 1024),
        name="pod_update",
    )(basis, sigma.reshape(1, K), snapshots)
    modes, values = pl.pallas_call(
        finish_kernel,
        out_shape=(jax.ShapeDtypeStruct((K, cols), jnp.float32),
                   jax.ShapeDtypeStruct((1, K), jnp.float32)),
        in_specs=[pl.BlockSpec(memory_space=pl.ANY), vmem],
        out_specs=(hbm, hbm),
        scratch_shapes=[pltpu.SemaphoreType.DMA((PARTS + 1,))],
        compiler_params=pltpu.CompilerParams(vmem_limit_bytes=1024 * 1024),
        name="write_out",
    )(modes, values)
    return modes, values.reshape(K)


def solution(mesh):
    placed = (P(None, AXES), P(), P(None, AXES))
    return jax.shard_map(
        per_device, mesh=mesh, in_specs=placed, out_specs=(P(None, AXES), P()), check_vma=False)
```

```python
import functools

import jax
import jax.numpy as jnp
from jax import lax
from jax.experimental import pallas as pl
from jax.experimental.pallas import tpu as pltpu
from jax.sharding import PartitionSpec as P

AXES = ("gx", "gy", "gz")
MESH = pl.DeviceIdType.MESH
HIGH = lax.Precision.HIGHEST
K, NEW = 32, 64

def dot(a, b): return jnp.dot(a, b, precision=HIGH, preferred_element_type=jnp.float32)
def dot_t(a, b): return lax.dot_general(a, b, (((1,), (1,)), ((), ())), precision=HIGH, preferred_element_type=jnp.float32)

def eliminate(N, U):
    nb = N.shape[0] // 8
    Nb = [N[8*i:8*i+8] for i in range(nb)]
    Ub = [U[8*i:8*i+8] for i in range(nb)]
    row = lax.broadcasted_iota(jnp.int32, (8, 128), 0)
    L = U.shape[1]
    def wide(x, width):
        return x[:, :width] if width <= 128 else jnp.concatenate([x] * (width // 128), axis=1)
    def column_splats(kb, Nb):
        return {(j, i): jnp.broadcast_to(Nb[i][:, 8*kb+j:8*kb+j+1], (8, 128))
                for j in range(8) for i in range(kb, nb)}
    out = []
    for kb in range(nb):
        X = ahead if kb else column_splats(0, Nb)
        ahead = {}
        scale = jnp.ones((8, 128), jnp.float32)
        for r in range(0, 8, 2):
            if r == 2 and kb < nb-1:
                ahead = column_splats(kb+1, Nb)
            spread = lambda x, s: jnp.broadcast_to(x[s:s+1], (8, x.shape[1]))
            a = spread(X[r, kb], r); b = spread(X[r+1, kb], r); c = spread(X[r+1, kb], r+1)
            det = a*c - b*b
            rdet = 1.0 / det
            ra = 1.0 / a
            f1 = {}; f2 = {}
            for i in range(kb, nb):
                f1[i] = (c*X[r, i] - b*X[r+1, i]) * rdet
                f2[i] = (a*X[r+1, i] - b*X[r, i]) * rdet
                if i == kb:
                    f1[i] = jnp.where(row > r+1, f1[i], jnp.where(row == r+1, b*ra, 0.0))
                    f2[i] = jnp.where(row > r+1, f2[i], 0.0)
            for j in range(r+2, 8):
                xa = spread(X[j, kb], r); xb = spread(X[j, kb], r+1)
                for i in range(kb, nb):
                    X[j, i] = X[j, i] - f1[i]*xa - f2[i]*xb
            for j in range(8 if ahead else 0):
                xa = spread(X[r, kb+1], j); xb = spread(X[r+1, kb+1], j)
                for i in range(kb+1, nb):
                    ahead[j, i] = ahead[j, i] - f1[i]*xa - f2[i]*xb
            na = spread(Nb[kb], r); nbb = spread(Nb[kb], r+1)
            ua = spread(Ub[kb], r); ub = spread(Ub[kb], r+1)
            for i in range(kb, nb):
                if kb < nb-1:
                    w = Nb[i].shape[1]
                    Nb[i] = Nb[i] - wide(f1[i], w)*na - wide(f2[i], w)*nbb
                Ub[i] = Ub[i] - wide(f1[i], L)*ua - wide(f2[i], L)*ub
            scale = jnp.where(row == r, lax.rsqrt(a), jnp.where(row == r+1, lax.rsqrt(det*ra), scale))
        out.append(Ub[kb] * wide(scale, L))
    return jnp.concatenate(out, axis=0)

def project(gbb, f):
    ft = f.T
    t = dot(gbb, f)
    c = 2.0*f - t
    ct = 2.0*ft - dot(ft, gbb)
    return ft, c, ct, dot(gbb, c) - f


def dense(ft, c, ct, h, gss, sigma_row):
    gram = gss + dot(jnp.concatenate([ct, -ft], 1), jnp.concatenate([h, c], 0))
    eye = lax.broadcasted_iota(jnp.int32, (K, K), 0) == lax.broadcasted_iota(jnp.int32, (K, K), 1)
    eye2 = lax.broadcasted_iota(jnp.int32, (NEW, NEW), 0) == lax.broadcasted_iota(jnp.int32, (NEW, NEW), 1)
    tau = jnp.sum(c*c, keepdims=True).reshape(1,1) + jnp.sum(jnp.where(eye2, gss, 0.0), keepdims=True).reshape(1,1) + jnp.sum(sigma_row*sigma_row, keepdims=True).reshape(1,1)
    rt = 1.0 / tau
    rs = lax.rsqrt(tau)
    sig2 = jnp.where(eye, sigma_row*sigma_row, 0.0)
    p = (sig2 + dot_t(c, c)) * rt
    cu = c
    c = c*rs; ct = ct*rs; gram = gram*rt
    cg = dot(c, gram); cgt = dot(gram, ct); g2 = dot(gram, gram)
    z32 = jnp.zeros((K, 32), jnp.float32); z64 = jnp.zeros((NEW, 32), jnp.float32)
    top = jnp.concatenate([p, c, z32, p, cg, z32], 1)
    bot = jnp.concatenate([cgt, gram, z64, cgt, g2, z64], 1)
    W = jnp.concatenate([top, bot], 0)
    VZ = top
    for step in range(4):
        V = VZ[:, :96]; Z = VZ[:, 128:224]
        N = dot_t(Z, V)
        VZ = eliminate(N, dot(V, W) if step < 3 else VZ)
    Y = VZ[:, :128]
    P = Y[:, :32]; w = Y[:, 32:96]
    Z = jnp.concatenate([P, dot(w, gram), z32], 1)
    N = dot_t(Z, Y)
    YS = dot(Y[:, :96], W[:, 128:])
    pb = P - dot(w, ct)
    U = jnp.concatenate([pb, w*rs, z32, Y, YS], 1)
    U = eliminate(N, U)
    ritz = jnp.sum(U[:, 128:224] * U[:, 256:352], axis=1, keepdims=True)
    values = jnp.sqrt(ritz * tau)
    return U[:, :128], values


CHUNK = 1024
LOAD = 2048
STACK = 2 * (K + NEW)


def tree_sum(values):
    while len(values) > 1:
        values = [a + b for a, b in zip(values[::2], values[1::2])] + values[len(values) // 2 * 2:]
    return values[0]


def split_gram(loads, basis_v, snap_v, split_v):
    full = None
    for i, pair in enumerate(loads):
        for copy in pair:
            copy.wait()
        at = slice(i * LOAD, (i + 1) * LOAD)
        for ref, low in ((basis_v, 0), (snap_v, K)):
            value = ref[:, at]
            high = value.astype(jnp.bfloat16)
            rest = (value - high.astype(jnp.float32)).astype(jnp.bfloat16)
            split_v[low:low + value.shape[0], at] = high
            split_v[K + NEW + low:K + NEW + low + value.shape[0], at] = rest
        both = split_v[:, at]
        term = lax.dot_general(both, both, (((1,), (1,)), ((), ())), preferred_element_type=jnp.float32)
        full = term if full is None else full + term
    half = K + NEW
    return (full[:half, :half] + full[half:, half:]) + (full[half:, :half] + full[:half, half:])


def update_kernel(na, ny, nz, basis_hbm, sigma_hbm, snap_hbm, left_ref, values_ref, split_v,
                basis_v, snap_v, packed, partner, chip, s1a, s1b, s2a, s2b, mids, gathered,
                sigma_ref, sigma_sem, load_sems, send_sems, recv_sems):
    x, y, z = lax.axis_index("gx"), lax.axis_index("gy"), lax.axis_index("gz")
    deep = na // 2
    level, core = x // 2, lax.rem(x, 2)
    own = 1 - core
    cols = basis_v.shape[1]
    loads = []
    for i in range(cols // LOAD):
        at = pl.ds(i * LOAD, LOAD)
        loads.append((
            pltpu.make_async_copy(basis_hbm.at[:, at], basis_v.at[:, at], load_sems.at[0, i]),
            pltpu.make_async_copy(snap_hbm.at[:, at], snap_v.at[:, at], load_sems.at[1, i]),
        ))
        for copy in loads[-1]:
            copy.start()

    sigma_load = pltpu.make_async_copy(sigma_hbm, sigma_ref, sigma_sem)
    sigma_load.start()

    here = y * nz + z

    def others_of(me, n):
        return [k + (k - me + n) // n for k in range(n - 1)]

    other = {"gx": x + 1 - 2 * core}
    plane = [{"gy": t // nz, "gz": lax.rem(t, nz)} for t in others_of(here, ny * nz)]
    line = [{"gx": 2 * t + core} for t in others_of(level, deep)]
    barrier = pltpu.get_barrier_semaphore()
    for device in [other] + plane + line:
        pl.semaphore_signal(barrier, inc=1, device_id=device, device_id_type=MESH)

    gram = split_gram(loads, basis_v, snap_v, split_v)
    half = K + NEW
    gap = jnp.zeros((K, 128 - half), jnp.float32)
    upper = jnp.concatenate([gram[:K], gap], axis=1)
    lower = jnp.concatenate([gram[K:2 * K, K:], gram[2 * K:, K:]], axis=1)
    rows = K // 2
    for i in range(2):
        packed[0, i] = upper[i * rows:(i + 1) * rows]
        packed[1, i] = lower[i * rows:(i + 1) * rows]

    pl.semaphore_wait(barrier, 1 + len(plane) + len(line))

    def send(phase, source, target, device):
        pltpu.make_async_remote_copy(
            src_ref=source, dst_ref=target, send_sem=send_sems.at[phase], recv_sem=recv_sems.at[phase],
            device_id=device, device_id_type=MESH).start()

    def arrive(phase, ref):
        pltpu.make_async_copy(ref, ref, recv_sems.at[phase]).wait()

    def sent(phase, ref):
        pltpu.make_async_copy(ref, ref, send_sems.at[phase]).wait()

    some_plane, some_line = pl.ds(0, len(plane)), pl.ds(0, len(line))
    send(0, packed.at[1 - own], partner, other)
    arrive(0, partner)
    for i in range(2):
        chip[i] = packed[own, i] + partner[i]
    order = [(k / len(plane), 0, k) for k in range(len(plane))] + [(k / len(line), 1, k) for k in range(len(line))]
    for _, which, k in sorted(order):
        if which == 0:
            send(1, chip.at[0], s1a.at[here], plane[k])
        else:
            send(2, chip.at[1], s1b.at[level], line[k])
    s1a[here] = chip[0]
    s1b[level] = chip[1]
    arrive(2, s1b.at[some_line])
    mids[1] = tree_sum([s1b[i] for i in range(deep)])
    for device in plane:
        send(3, mids.at[1], s2b.at[here], device)
    s2b[here] = mids[1]
    arrive(1, s1a.at[some_plane])
    mids[0] = tree_sum([s1a[i] for i in range(ny * nz)])
    for device in line:
        send(4, mids.at[0], s2a.at[level], device)
    s2a[level] = mids[0]
    arrive(4, s2a.at[some_line])
    gathered[own, 0] = tree_sum([s2a[i] for i in range(deep)])
    arrive(3, s2b.at[some_plane])
    gathered[own, 1] = tree_sum([s2b[i] for i in range(ny * nz)])
    send(5, gathered.at[own], gathered.at[own], other)
    scale = 1.0 / (cols * na * ny * nz)

    @pl.when(core == 0)
    def _():
        arrive(5, gathered.at[0])

    upper = jnp.concatenate([gathered[0, 0], gathered[0, 1]], axis=0) * scale
    projected = project(upper[:, :K], upper[:, K:K + NEW])

    @pl.when(core == 1)
    def _():
        arrive(5, gathered.at[1])

    sigma_load.wait()
    lower = jnp.concatenate([gathered[1, 0], gathered[1, 1]], axis=0) * scale
    gss = jnp.concatenate([lower[:, :NEW], lower[:, NEW:]], axis=0)
    coef, values = dense(*projected, gss, sigma_ref[...])
    eye = lax.broadcasted_iota(jnp.int32, (K, K), 0) == lax.broadcasted_iota(jnp.int32, (K, K), 1)
    values_ref[...] = jnp.sum(jnp.where(eye, values, 0.0), axis=0, keepdims=True)
    coef = coef[:, :K + NEW]
    high = coef.astype(jnp.bfloat16).astype(jnp.float32)
    rest = coef - high
    left_ref[...] = jnp.concatenate([
        jnp.concatenate([high, high], axis=1), jnp.concatenate([rest, rest], axis=1)], axis=0).astype(jnp.bfloat16)
    sent(0, partner)
    sent(1, s1a.at[some_plane])
    sent(2, s1b.at[some_line])
    sent(3, s2b.at[some_plane])
    sent(4, s2a.at[some_line])
    sent(5, partner)


def finish_kernel(left_ref, values_ref, split_ref, modes_hbm, values_hbm, modes_v, sems):
    cols = modes_hbm.shape[1]
    chunks = cols // CHUNK
    left = left_ref[...]
    copies = [pltpu.make_async_copy(values_ref, values_hbm, sems.at[chunks])]
    copies[0].start()
    for i in range(chunks):
        at = pl.ds(i * CHUNK, CHUNK)
        both = jnp.dot(left, split_ref[:, at], preferred_element_type=jnp.float32)
        modes_v[:, at] = both[:K] + both[K:]
        copies.append(pltpu.make_async_copy(modes_v.at[:, at], modes_hbm.at[:, at], sems.at[i]))
        copies[-1].start()
    for copy in copies:
        copy.wait()


def per_device(basis, sigma, snapshots):
    na, ny, nz = (lax.axis_size(a) for a in AXES)
    cols = basis.shape[1]
    vmem = pl.BlockSpec(memory_space=pltpu.VMEM)
    hbm = pl.BlockSpec(memory_space=pltpu.HBM)
    quarter = (K // 2, 128)
    def slots(*count):
        return pltpu.VMEM(count + quarter, jnp.float32)
    left, values, split = pl.pallas_call(
        functools.partial(update_kernel, na, ny, nz),
        out_shape=(jax.ShapeDtypeStruct((2 * K, STACK), jnp.bfloat16),
                   jax.ShapeDtypeStruct((1, K), jnp.float32),
                   jax.ShapeDtypeStruct((STACK, cols), jnp.bfloat16)),
        in_specs=[hbm, hbm, hbm],
        out_specs=(vmem, vmem, vmem),
        scratch_shapes=[
            pltpu.VMEM((K, cols), jnp.float32),
            pltpu.VMEM((NEW, cols), jnp.float32),
            slots(2, 2), slots(2), slots(2),
            slots(ny * nz), slots(na // 2), slots(na // 2), slots(ny * nz), slots(2), slots(2, 2),
            pltpu.VMEM((1, K), jnp.float32),
            pltpu.SemaphoreType.DMA,
            pltpu.SemaphoreType.DMA((2, cols // LOAD)),
            pltpu.SemaphoreType.DMA((6,)),
            pltpu.SemaphoreType.DMA((6,)),
        ],
        compiler_params=pltpu.CompilerParams(
            collective_id=0, has_side_effects=True, vmem_limit_bytes=32 * 1024 * 1024),
        name="pod_update",
    )(*(pltpu.with_memory_space_constraint(value, pltpu.HBM)
        for value in (basis, sigma.reshape(1, K), snapshots)))
    modes, values = pl.pallas_call(
        finish_kernel,
        out_shape=(jax.ShapeDtypeStruct((K, cols), jnp.float32),
                   jax.ShapeDtypeStruct((1, K), jnp.float32)),
        in_specs=[vmem, vmem, vmem],
        out_specs=(hbm, hbm),
        scratch_shapes=[pltpu.VMEM((K, cols), jnp.float32), pltpu.SemaphoreType.DMA((cols // CHUNK + 1,))],
        compiler_params=pltpu.CompilerParams(vmem_limit_bytes=8 * 1024 * 1024),
        name="modes_product",
    )(left, values, split)
    return modes, values.reshape(K)


def solution(mesh):
    placed = (P(None, AXES), P(), P(None, AXES))
    return jax.shard_map(
        per_device, mesh=mesh, in_specs=placed, out_specs=(P(None, AXES), P()), check_vma=False)
```

```python
import functools

import jax
import jax.numpy as jnp
from jax import lax
from jax.experimental import pallas as pl
from jax.experimental.pallas import tpu as pltpu
from jax.sharding import PartitionSpec as P

AXES = ("gx", "gy", "gz")
MESH = pl.DeviceIdType.MESH
HIGH = lax.Precision.HIGHEST
K, NEW = 32, 64

def dot(a, b): return jnp.dot(a, b, precision=HIGH, preferred_element_type=jnp.float32)
def dot_t(a, b): return lax.dot_general(a, b, (((1,), (1,)), ((), ())), precision=HIGH, preferred_element_type=jnp.float32)

def eliminate(N, U):
    nb = N.shape[0] // 8
    Nb = [N[8*i:8*i+8] for i in range(nb)]
    Ub = [U[8*i:8*i+8] for i in range(nb)]
    row = lax.broadcasted_iota(jnp.int32, (8, 128), 0)
    L = U.shape[1]
    def wide(x, width):
        return x[:, :width] if width <= 128 else jnp.concatenate([x] * (width // 128), axis=1)
    def column_splats(kb, Nb):
        return {(j, i): jnp.broadcast_to(Nb[i][:, 8*kb+j:8*kb+j+1], (8, 128))
                for j in range(8) for i in range(kb, nb)}
    out = []
    for kb in range(nb):
        X = ahead if kb else column_splats(0, Nb)
        ahead = {}
        scale = jnp.ones((8, 128), jnp.float32)
        for r in range(0, 8, 2):
            if r == 2 and kb < nb-1:
                ahead = column_splats(kb+1, Nb)
            spread = lambda x, s: jnp.broadcast_to(x[s:s+1], (8, x.shape[1]))
            a = spread(X[r, kb], r); b = spread(X[r+1, kb], r); c = spread(X[r+1, kb], r+1)
            det = a*c - b*b
            rdet = 1.0 / det
            ra = 1.0 / a
            f1 = {}; f2 = {}
            for i in range(kb, nb):
                f1[i] = (c*X[r, i] - b*X[r+1, i]) * rdet
                f2[i] = (a*X[r+1, i] - b*X[r, i]) * rdet
                if i == kb:
                    f1[i] = jnp.where(row > r+1, f1[i], jnp.where(row == r+1, b*ra, 0.0))
                    f2[i] = jnp.where(row > r+1, f2[i], 0.0)
            for j in range(r+2, 8):
                xa = spread(X[j, kb], r); xb = spread(X[j, kb], r+1)
                for i in range(kb, nb):
                    X[j, i] = X[j, i] - f1[i]*xa - f2[i]*xb
            for j in range(8 if ahead else 0):
                xa = spread(X[r, kb+1], j); xb = spread(X[r+1, kb+1], j)
                for i in range(kb+1, nb):
                    ahead[j, i] = ahead[j, i] - f1[i]*xa - f2[i]*xb
            na = spread(Nb[kb], r); nbb = spread(Nb[kb], r+1)
            ua = spread(Ub[kb], r); ub = spread(Ub[kb], r+1)
            for i in range(kb, nb):
                if kb < nb-1:
                    w = Nb[i].shape[1]
                    Nb[i] = Nb[i] - wide(f1[i], w)*na - wide(f2[i], w)*nbb
                Ub[i] = Ub[i] - wide(f1[i], L)*ua - wide(f2[i], L)*ub
            scale = jnp.where(row == r, lax.rsqrt(a), jnp.where(row == r+1, lax.rsqrt(det*ra), scale))
        out.append(Ub[kb] * wide(scale, L))
    return jnp.concatenate(out, axis=0)

def project(gbb, f):
    ft = f.T
    t = dot(gbb, f)
    c = 2.0*f - t
    ct = 2.0*ft - dot(ft, gbb)
    return ft, c, ct, dot(gbb, c) - f


def dense(ft, c, ct, h, gss, sigma_row):
    gram = gss + dot(jnp.concatenate([ct, -ft], 1), jnp.concatenate([h, c], 0))
    eye = lax.broadcasted_iota(jnp.int32, (K, K), 0) == lax.broadcasted_iota(jnp.int32, (K, K), 1)
    eye2 = lax.broadcasted_iota(jnp.int32, (NEW, NEW), 0) == lax.broadcasted_iota(jnp.int32, (NEW, NEW), 1)
    tau = jnp.sum(c*c, keepdims=True).reshape(1,1) + jnp.sum(jnp.where(eye2, gss, 0.0), keepdims=True).reshape(1,1) + jnp.sum(sigma_row*sigma_row, keepdims=True).reshape(1,1)
    rt = 1.0 / tau
    rs = lax.rsqrt(tau)
    sig2 = jnp.where(eye, sigma_row*sigma_row, 0.0)
    p = (sig2 + dot_t(c, c)) * rt
    cu = c
    c = c*rs; ct = ct*rs; gram = gram*rt
    cg = dot(c, gram); cgt = dot(gram, ct); g2 = dot(gram, gram)
    z32 = jnp.zeros((K, 32), jnp.float32); z64 = jnp.zeros((NEW, 32), jnp.float32)
    top = jnp.concatenate([p, c, z32, p, cg, z32], 1)
    bot = jnp.concatenate([cgt, gram, z64, cgt, g2, z64], 1)
    W = jnp.concatenate([top, bot], 0)
    VZ = top
    for step in range(4):
        V = VZ[:, :96]; Z = VZ[:, 128:224]
        N = dot_t(Z, V)
        VZ = eliminate(N, dot(V, W) if step < 3 else VZ)
    Y = VZ[:, :128]
    P = Y[:, :32]; w = Y[:, 32:96]
    Z = jnp.concatenate([P, dot(w, gram), z32], 1)
    N = dot_t(Z, Y)
    YS = dot(Y[:, :96], W[:, 128:])
    pb = P - dot(w, ct)
    U = jnp.concatenate([pb, w*rs, z32, Y, YS], 1)
    U = eliminate(N, U)
    ritz = jnp.sum(U[:, 128:224] * U[:, 256:352], axis=1, keepdims=True)
    values = jnp.sqrt(ritz * tau)
    return U[:, :128], values


CHUNK = 1024
LOAD = 4096
STACK = 2 * (K + NEW)


def tree_sum(values):
    while len(values) > 1:
        values = [a + b for a, b in zip(values[::2], values[1::2])] + values[len(values) // 2 * 2:]
    return values[0]


def split_gram(load_sems, basis_v, snap_v, split_v):
    def step(i, full):
        at = pl.ds(pl.multiple_of(i * LOAD, LOAD), LOAD)
        for which, ref, low in ((0, basis_v, 0), (1, snap_v, K)):
            pltpu.make_async_copy(ref.at[:, at], ref.at[:, at], load_sems.at[which, i]).wait()
            value = ref[:, at]
            high = value.astype(jnp.bfloat16)
            rest = (value - high.astype(jnp.float32)).astype(jnp.bfloat16)
            split_v[low:low + value.shape[0], at] = high
            split_v[K + NEW + low:K + NEW + low + value.shape[0], at] = rest
        both = split_v[:, at]
        return full + lax.dot_general(both, both, (((1,), (1,)), ((), ())), preferred_element_type=jnp.float32)

    full = lax.fori_loop(0, basis_v.shape[1] // LOAD, step, jnp.zeros((STACK, STACK), jnp.float32))
    half = K + NEW
    return (full[:half, :half] + full[half:, half:]) + (full[half:, :half] + full[:half, half:])


def update_kernel(na, ny, nz, basis_hbm, sigma_hbm, snap_hbm, left_ref, values_ref, split_v,
                basis_v, snap_v, packed, partner, chip, s1a, s1b, s2a, s2b, mids, gathered,
                sigma_ref, sigma_sem, load_sems, send_sems, recv_sems):
    x, y, z = lax.axis_index("gx"), lax.axis_index("gy"), lax.axis_index("gz")
    deep = na // 2
    level, core = x // 2, lax.rem(x, 2)
    own = 1 - core
    cols = basis_v.shape[1]
    loads = []
    for i in range(cols // LOAD):
        at = pl.ds(i * LOAD, LOAD)
        loads.append((
            pltpu.make_async_copy(basis_hbm.at[:, at], basis_v.at[:, at], load_sems.at[0, i]),
            pltpu.make_async_copy(snap_hbm.at[:, at], snap_v.at[:, at], load_sems.at[1, i]),
        ))
        for copy in loads[-1]:
            copy.start()

    sigma_load = pltpu.make_async_copy(sigma_hbm, sigma_ref, sigma_sem)
    sigma_load.start()

    here = y * nz + z

    def others_of(me, n):
        return [k + (k - me + n) // n for k in range(n - 1)]

    other = {"gx": x + 1 - 2 * core}
    plane = [{"gy": t // nz, "gz": lax.rem(t, nz)} for t in others_of(here, ny * nz)]
    line = [{"gx": 2 * t + core} for t in others_of(level, deep)]
    def hops(d, n):
        return min(d, n - d)

    far = [(hops(dy, ny) + hops(dz, nz), {"gy": lax.rem(y + dy, ny), "gz": lax.rem(z + dz, nz)})
           for dy in range(ny) for dz in range(nz) if dy or dz]
    far += [(hops(d, deep), {"gx": lax.rem(level + d, deep) * 2 + core}) for d in range(1, deep)]
    far = [device for _, device in sorted(far, key=lambda entry: -entry[0])]
    barrier = pltpu.get_barrier_semaphore()
    for device in far + [other]:
        pl.semaphore_signal(barrier, inc=1, device_id=device, device_id_type=MESH)

    gram = split_gram(load_sems, basis_v, snap_v, split_v)
    half = K + NEW
    gap = jnp.zeros((K, 128 - half), jnp.float32)
    upper = jnp.concatenate([gram[:K], gap], axis=1)
    lower = jnp.concatenate([gram[K:2 * K, K:], gram[2 * K:, K:]], axis=1)
    rows = K // 2
    for i in range(2):
        packed[0, i] = upper[i * rows:(i + 1) * rows]
        packed[1, i] = lower[i * rows:(i + 1) * rows]

    pl.semaphore_wait(barrier, 1 + len(plane) + len(line))

    def send(phase, source, target, device):
        pltpu.make_async_remote_copy(
            src_ref=source, dst_ref=target, send_sem=send_sems.at[phase], recv_sem=recv_sems.at[phase],
            device_id=device, device_id_type=MESH).start()

    def arrive(phase, ref):
        pltpu.make_async_copy(ref, ref, recv_sems.at[phase]).wait()

    def sent(phase, ref):
        pltpu.make_async_copy(ref, ref, send_sems.at[phase]).wait()

    some_plane, some_line = pl.ds(0, len(plane)), pl.ds(0, len(line))
    send(0, packed.at[1 - own], partner, other)
    arrive(0, partner)
    for i in range(2):
        chip[i] = packed[own, i] + partner[i]
    order = [(k / len(plane), 0, k) for k in range(len(plane))] + [(k / len(line), 1, k) for k in range(len(line))]
    for _, which, k in sorted(order):
        if which == 0:
            send(1, chip.at[0], s1a.at[here], plane[k])
        else:
            send(2, chip.at[1], s1b.at[level], line[k])
    s1a[here] = chip[0]
    s1b[level] = chip[1]
    arrive(2, s1b.at[some_line])
    mids[1] = tree_sum([s1b[i] for i in range(deep)])
    for device in plane:
        send(3, mids.at[1], s2b.at[here], device)
    s2b[here] = mids[1]
    arrive(1, s1a.at[some_plane])
    mids[0] = tree_sum([s1a[i] for i in range(ny * nz)])
    for device in line:
        send(4, mids.at[0], s2a.at[level], device)
    s2a[level] = mids[0]
    arrive(4, s2a.at[some_line])
    gathered[own, 0] = tree_sum([s2a[i] for i in range(deep)])
    arrive(3, s2b.at[some_plane])
    gathered[own, 1] = tree_sum([s2b[i] for i in range(ny * nz)])
    send(5, gathered.at[own], gathered.at[own], other)
    scale = 1.0 / (cols * na * ny * nz)

    @pl.when(core == 0)
    def _():
        arrive(5, gathered.at[0])

    upper = jnp.concatenate([gathered[0, 0], gathered[0, 1]], axis=0) * scale
    projected = project(upper[:, :K], upper[:, K:K + NEW])

    @pl.when(core == 1)
    def _():
        arrive(5, gathered.at[1])

    sigma_load.wait()
    lower = jnp.concatenate([gathered[1, 0], gathered[1, 1]], axis=0) * scale
    gss = jnp.concatenate([lower[:, :NEW], lower[:, NEW:]], axis=0)
    coef, values = dense(*projected, gss, sigma_ref[...])
    eye = lax.broadcasted_iota(jnp.int32, (K, K), 0) == lax.broadcasted_iota(jnp.int32, (K, K), 1)
    values_ref[...] = jnp.sum(jnp.where(eye, values, 0.0), axis=0, keepdims=True)
    coef = coef[:, :K + NEW]
    high = coef.astype(jnp.bfloat16).astype(jnp.float32)
    rest = coef - high
    left_ref[...] = jnp.concatenate([
        jnp.concatenate([high, high], axis=1), jnp.concatenate([rest, rest], axis=1)], axis=0).astype(jnp.bfloat16)
    sent(0, partner)
    sent(1, s1a.at[some_plane])
    sent(2, s1b.at[some_line])
    sent(3, s2b.at[some_plane])
    sent(4, s2a.at[some_line])
    sent(5, partner)


def finish_kernel(left_ref, values_ref, split_ref, modes_hbm, values_hbm, modes_v, sems):
    cols = modes_hbm.shape[1]
    chunks = cols // CHUNK
    left = left_ref[...]
    copies = [pltpu.make_async_copy(values_ref, values_hbm, sems.at[chunks])]
    copies[0].start()
    for i in range(chunks):
        at = pl.ds(i * CHUNK, CHUNK)
        both = jnp.dot(left, split_ref[:, at], preferred_element_type=jnp.float32)
        modes_v[:, at] = both[:K] + both[K:]
        copies.append(pltpu.make_async_copy(modes_v.at[:, at], modes_hbm.at[:, at], sems.at[i]))
        copies[-1].start()
    for copy in copies:
        copy.wait()


def per_device(basis, sigma, snapshots):
    na, ny, nz = (lax.axis_size(a) for a in AXES)
    cols = basis.shape[1]
    vmem = pl.BlockSpec(memory_space=pltpu.VMEM)
    hbm = pl.BlockSpec(memory_space=pltpu.HBM)
    quarter = (K // 2, 128)
    def slots(*count):
        return pltpu.VMEM(count + quarter, jnp.float32)
    left, values, split = pl.pallas_call(
        functools.partial(update_kernel, na, ny, nz),
        out_shape=(jax.ShapeDtypeStruct((2 * K, STACK), jnp.bfloat16),
                   jax.ShapeDtypeStruct((1, K), jnp.float32),
                   jax.ShapeDtypeStruct((STACK, cols), jnp.bfloat16)),
        in_specs=[hbm, hbm, hbm],
        out_specs=(vmem, vmem, vmem),
        scratch_shapes=[
            pltpu.VMEM((K, cols), jnp.float32),
            pltpu.VMEM((NEW, cols), jnp.float32),
            slots(2, 2), slots(2), slots(2),
            slots(ny * nz), slots(na // 2), slots(na // 2), slots(ny * nz), slots(2), slots(2, 2),
            pltpu.VMEM((1, K), jnp.float32),
            pltpu.SemaphoreType.DMA,
            pltpu.SemaphoreType.DMA((2, cols // LOAD)),
            pltpu.SemaphoreType.DMA((6,)),
            pltpu.SemaphoreType.DMA((6,)),
        ],
        compiler_params=pltpu.CompilerParams(
            collective_id=0, has_side_effects=True, vmem_limit_bytes=32 * 1024 * 1024),
        name="pod_update",
    )(*(pltpu.with_memory_space_constraint(value, pltpu.HBM)
        for value in (basis, sigma.reshape(1, K), snapshots)))
    modes, values = pl.pallas_call(
        finish_kernel,
        out_shape=(jax.ShapeDtypeStruct((K, cols), jnp.float32),
                   jax.ShapeDtypeStruct((1, K), jnp.float32)),
        in_specs=[vmem, vmem, vmem],
        out_specs=(hbm, hbm),
        scratch_shapes=[pltpu.VMEM((K, cols), jnp.float32), pltpu.SemaphoreType.DMA((cols // CHUNK + 1,))],
        compiler_params=pltpu.CompilerParams(vmem_limit_bytes=8 * 1024 * 1024),
        name="modes_product",
    )(left, values, split)
    return modes, values.reshape(K)


def solution(mesh):
    placed = (P(None, AXES), P(), P(None, AXES))
    return jax.shard_map(
        per_device, mesh=mesh, in_specs=placed, out_specs=(P(None, AXES), P()), check_vma=False)
```

```python
import functools

import jax
import jax.numpy as jnp
from jax import lax
from jax.experimental import pallas as pl
from jax.experimental.pallas import tpu as pltpu
from jax.sharding import PartitionSpec as P

AXES = ("gx", "gy", "gz")
MESH = pl.DeviceIdType.MESH
HIGH = lax.Precision.HIGHEST
K, NEW = 32, 64

def dot(a, b): return jnp.dot(a, b, precision=HIGH, preferred_element_type=jnp.float32)
def dot_t(a, b): return lax.dot_general(a, b, (((1,), (1,)), ((), ())), precision=HIGH, preferred_element_type=jnp.float32)

def eliminate(N, U):
    nb = N.shape[0] // 8
    Nb = [N[8*i:8*i+8] for i in range(nb)]
    Ub = [U[8*i:8*i+8] for i in range(nb)]
    row = lax.broadcasted_iota(jnp.int32, (8, 128), 0)
    L = U.shape[1]
    def wide(x, width):
        return x[:, :width] if width <= 128 else jnp.concatenate([x] * (width // 128), axis=1)
    def column_splats(kb, Nb):
        return {(j, i): jnp.broadcast_to(Nb[i][:, 8*kb+j:8*kb+j+1], (8, 128))
                for j in range(8) for i in range(kb, nb)}
    out = []
    for kb in range(nb):
        X = ahead if kb else column_splats(0, Nb)
        ahead = {}
        scale = jnp.ones((8, 128), jnp.float32)
        for r in range(0, 8, 2):
            if r == 2 and kb < nb-1:
                ahead = column_splats(kb+1, Nb)
            spread = lambda x, s: jnp.broadcast_to(x[s:s+1], (8, x.shape[1]))
            a = spread(X[r, kb], r); b = spread(X[r+1, kb], r); c = spread(X[r+1, kb], r+1)
            det = a*c - b*b
            rdet = 1.0 / det
            ra = 1.0 / a
            f1 = {}; f2 = {}
            for i in range(kb, nb):
                f1[i] = (c*X[r, i] - b*X[r+1, i]) * rdet
                f2[i] = (a*X[r+1, i] - b*X[r, i]) * rdet
                if i == kb:
                    f1[i] = jnp.where(row > r+1, f1[i], jnp.where(row == r+1, b*ra, 0.0))
                    f2[i] = jnp.where(row > r+1, f2[i], 0.0)
            for j in range(r+2, 8):
                xa = spread(X[j, kb], r); xb = spread(X[j, kb], r+1)
                for i in range(kb, nb):
                    X[j, i] = X[j, i] - (f1[i]*xa + f2[i]*xb)
            for j in range(8 if ahead else 0):
                xa = spread(X[r, kb+1], j); xb = spread(X[r+1, kb+1], j)
                for i in range(kb+1, nb):
                    ahead[j, i] = ahead[j, i] - (f1[i]*xa + f2[i]*xb)
            na = spread(Nb[kb], r); nbb = spread(Nb[kb], r+1)
            ua = spread(Ub[kb], r); ub = spread(Ub[kb], r+1)
            for i in range(kb, nb):
                if kb < nb-1 and (r < 2 or kb < nb-2) and (i > kb or r < 6):
                    w = Nb[i].shape[1]
                    Nb[i] = Nb[i] - wide(f1[i], w)*na - wide(f2[i], w)*nbb
                Ub[i] = Ub[i] - wide(f1[i], L)*ua - wide(f2[i], L)*ub
            scale = jnp.where(row == r, lax.rsqrt(a), jnp.where(row == r+1, lax.rsqrt(det*ra), scale))
        out.append(Ub[kb] * wide(scale, L))
    return jnp.concatenate(out, axis=0)

def project(gbb, f):
    ft = f.T
    t = dot(gbb, f)
    c = 2.0*f - t
    ct = 2.0*ft - dot(ft, gbb)
    return ft, c, ct, dot(gbb, c) - f


def dense(ft, c, ct, h, gss, sigma_row):
    gram = gss + dot(jnp.concatenate([ct, -ft], 1), jnp.concatenate([h, c], 0))
    eye = lax.broadcasted_iota(jnp.int32, (K, K), 0) == lax.broadcasted_iota(jnp.int32, (K, K), 1)
    eye2 = lax.broadcasted_iota(jnp.int32, (NEW, NEW), 0) == lax.broadcasted_iota(jnp.int32, (NEW, NEW), 1)
    tau = jnp.sum(c*c, keepdims=True).reshape(1,1) + jnp.sum(jnp.where(eye2, gss, 0.0), keepdims=True).reshape(1,1) + jnp.sum(sigma_row*sigma_row, keepdims=True).reshape(1,1)
    rt = 1.0 / tau
    rs = lax.rsqrt(tau)
    sig2 = jnp.where(eye, sigma_row*sigma_row, 0.0)
    p = (sig2 + dot_t(c, c)) * rt
    cu = c
    c = c*rs; ct = ct*rs; gram = gram*rt
    cg = dot(c, gram); cgt = dot(gram, ct); g2 = dot(gram, gram)
    z32 = jnp.zeros((K, 32), jnp.float32); z64 = jnp.zeros((NEW, 32), jnp.float32)
    top = jnp.concatenate([p, c, z32, p, cg, z32], 1)
    bot = jnp.concatenate([cgt, gram, z64, cgt, g2, z64], 1)
    W = jnp.concatenate([top, bot], 0)
    VZ = top
    for step in range(4):
        V = VZ[:, :96]; Z = VZ[:, 128:224]
        N = dot_t(Z, V)
        VZ = eliminate(N, dot(V, W) if step < 3 else VZ)
    Y = VZ[:, :128]
    P = Y[:, :32]; w = Y[:, 32:96]
    Z = jnp.concatenate([P, dot(w, gram), z32], 1)
    N = dot_t(Z, Y)
    YS = dot(Y[:, :96], W[:, 128:])
    pb = P - dot(w, ct)
    U = jnp.concatenate([pb, w*rs, z32, Y, YS], 1)
    U = eliminate(N, U)
    ritz = jnp.sum(U[:, 128:224] * U[:, 256:352], axis=1, keepdims=True)
    values = jnp.sqrt(ritz * tau)
    return U[:, :128], values


CHUNK = 1024
LOAD = 4096
STACK = 2 * (K + NEW)


def tree_sum(values):
    while len(values) > 1:
        values = [a + b for a, b in zip(values[::2], values[1::2])] + values[len(values) // 2 * 2:]
    return values[0]


def split_gram(load_sems, basis_v, snap_v, split_v):
    def step(i, full):
        at = pl.ds(pl.multiple_of(i * LOAD, LOAD), LOAD)
        for which, ref, low in ((0, basis_v, 0), (1, snap_v, K)):
            pltpu.make_async_copy(ref.at[:, at], ref.at[:, at], load_sems.at[which, i]).wait()
            value = ref[:, at]
            high = value.astype(jnp.bfloat16)
            rest = (value - high.astype(jnp.float32)).astype(jnp.bfloat16)
            split_v[low:low + value.shape[0], at] = high
            split_v[K + NEW + low:K + NEW + low + value.shape[0], at] = rest
        both = split_v[:, at]
        return full + lax.dot_general(both, both, (((1,), (1,)), ((), ())), preferred_element_type=jnp.float32)

    full = lax.fori_loop(0, basis_v.shape[1] // LOAD, step, jnp.zeros((STACK, STACK), jnp.float32))
    half = K + NEW
    return (full[:half, :half] + full[half:, half:]) + (full[half:, :half] + full[:half, half:])


def update_kernel(na, ny, nz, basis_hbm, sigma_hbm, snap_hbm, left_ref, values_ref, split_v,
                basis_v, snap_v, packed, partner, chip, s1a, s1b, s2a, s2b, mids, gathered,
                sigma_ref, sigma_sem, load_sems, send_sems, recv_sems):
    x, y, z = lax.axis_index("gx"), lax.axis_index("gy"), lax.axis_index("gz")
    deep = na // 2
    level, core = x // 2, lax.rem(x, 2)
    own = 1 - core
    cols = basis_v.shape[1]
    loads = []
    for i in range(cols // LOAD):
        at = pl.ds(i * LOAD, LOAD)
        loads.append((
            pltpu.make_async_copy(basis_hbm.at[:, at], basis_v.at[:, at], load_sems.at[0, i]),
            pltpu.make_async_copy(snap_hbm.at[:, at], snap_v.at[:, at], load_sems.at[1, i]),
        ))
        for copy in loads[-1]:
            copy.start()

    sigma_load = pltpu.make_async_copy(sigma_hbm, sigma_ref, sigma_sem)
    sigma_load.start()

    here = y * nz + z

    def others_of(me, n):
        return [k + (k - me + n) // n for k in range(n - 1)]

    other = {"gx": x + 1 - 2 * core}
    plane = [{"gy": t // nz, "gz": lax.rem(t, nz)} for t in others_of(here, ny * nz)]
    line = [{"gx": 2 * t + core} for t in others_of(level, deep)]
    def hops(d, n):
        return min(d, n - d)

    far = [(hops(dy, ny) + hops(dz, nz), {"gy": lax.rem(y + dy, ny), "gz": lax.rem(z + dz, nz)})
           for dy in range(ny) for dz in range(nz) if dy or dz]
    far += [(hops(d, deep), {"gx": lax.rem(level + d, deep) * 2 + core}) for d in range(1, deep)]
    far = [device for _, device in sorted(far, key=lambda entry: -entry[0])]
    barrier = pltpu.get_barrier_semaphore()
    for device in far + [other]:
        pl.semaphore_signal(barrier, inc=1, device_id=device, device_id_type=MESH)

    gram = split_gram(load_sems, basis_v, snap_v, split_v)
    half = K + NEW
    gap = jnp.zeros((K, 128 - half), jnp.float32)
    upper = jnp.concatenate([gram[:K], gap], axis=1)
    lower = jnp.concatenate([gram[K:2 * K, K:], gram[2 * K:, K:]], axis=1)
    rows = K // 2
    for i in range(2):
        packed[0, i] = upper[i * rows:(i + 1) * rows]
        packed[1, i] = lower[i * rows:(i + 1) * rows]

    pl.semaphore_wait(barrier, 1 + len(plane) + len(line))

    def send(phase, source, target, device):
        pltpu.make_async_remote_copy(
            src_ref=source, dst_ref=target, send_sem=send_sems.at[phase], recv_sem=recv_sems.at[phase],
            device_id=device, device_id_type=MESH).start()

    def arrive(phase, ref):
        pltpu.make_async_copy(ref, ref, recv_sems.at[phase]).wait()

    def sent(phase, ref):
        pltpu.make_async_copy(ref, ref, send_sems.at[phase]).wait()

    some_plane, some_line = pl.ds(0, len(plane)), pl.ds(0, len(line))
    send(0, packed.at[1 - own], partner, other)
    arrive(0, partner)
    for i in range(2):
        chip[i] = packed[own, i] + partner[i]
    order = [(k / len(plane), 0, k) for k in range(len(plane))] + [(k / len(line), 1, k) for k in range(len(line))]
    for _, which, k in sorted(order):
        if which == 0:
            send(1, chip.at[0], s1a.at[here], plane[k])
        else:
            send(2, chip.at[1], s1b.at[level], line[k])
    s1a[here] = chip[0]
    s1b[level] = chip[1]
    arrive(2, s1b.at[some_line])
    mids[1] = tree_sum([s1b[i] for i in range(deep)])
    for device in plane:
        send(3, mids.at[1], s2b.at[here], device)
    s2b[here] = mids[1]
    arrive(1, s1a.at[some_plane])
    mids[0] = tree_sum([s1a[i] for i in range(ny * nz)])
    for device in line:
        send(4, mids.at[0], s2a.at[level], device)
    s2a[level] = mids[0]
    arrive(4, s2a.at[some_line])
    gathered[own, 0] = tree_sum([s2a[i] for i in range(deep)])
    arrive(3, s2b.at[some_plane])
    gathered[own, 1] = tree_sum([s2b[i] for i in range(ny * nz)])
    send(5, gathered.at[own], gathered.at[own], other)
    scale = 1.0 / (cols * na * ny * nz)

    @pl.when(core == 0)
    def _():
        arrive(5, gathered.at[0])

    upper = jnp.concatenate([gathered[0, 0], gathered[0, 1]], axis=0) * scale
    projected = project(upper[:, :K], upper[:, K:K + NEW])

    @pl.when(core == 1)
    def _():
        arrive(5, gathered.at[1])

    sigma_load.wait()
    lower = jnp.concatenate([gathered[1, 0], gathered[1, 1]], axis=0) * scale
    gss = jnp.concatenate([lower[:, :NEW], lower[:, NEW:]], axis=0)
    coef, values = dense(*projected, gss, sigma_ref[...])
    eye = lax.broadcasted_iota(jnp.int32, (K, K), 0) == lax.broadcasted_iota(jnp.int32, (K, K), 1)
    values_ref[...] = jnp.sum(jnp.where(eye, values, 0.0), axis=0, keepdims=True)
    coef = coef[:, :K + NEW]
    high = coef.astype(jnp.bfloat16).astype(jnp.float32)
    rest = coef - high
    left_ref[...] = jnp.concatenate([
        jnp.concatenate([high, high], axis=1), jnp.concatenate([rest, rest], axis=1)], axis=0).astype(jnp.bfloat16)
    sent(0, partner)
    sent(1, s1a.at[some_plane])
    sent(2, s1b.at[some_line])
    sent(3, s2b.at[some_plane])
    sent(4, s2a.at[some_line])
    sent(5, partner)


def finish_kernel(left_ref, values_ref, split_ref, modes_hbm, values_hbm, modes_v, sems):
    cols = modes_hbm.shape[1]
    chunks = cols // CHUNK
    left = left_ref[...]
    copies = [pltpu.make_async_copy(values_ref, values_hbm, sems.at[chunks])]
    copies[0].start()
    for i in range(chunks):
        at = pl.ds(i * CHUNK, CHUNK)
        both = jnp.dot(left, split_ref[:, at], preferred_element_type=jnp.float32)
        modes_v[:, at] = both[:K] + both[K:]
        copies.append(pltpu.make_async_copy(modes_v.at[:, at], modes_hbm.at[:, at], sems.at[i]))
        copies[-1].start()
    for copy in copies:
        copy.wait()


def per_device(basis, sigma, snapshots):
    na, ny, nz = (lax.axis_size(a) for a in AXES)
    cols = basis.shape[1]
    vmem = pl.BlockSpec(memory_space=pltpu.VMEM)
    hbm = pl.BlockSpec(memory_space=pltpu.HBM)
    quarter = (K // 2, 128)
    def slots(*count):
        return pltpu.VMEM(count + quarter, jnp.float32)
    left, values, split = pl.pallas_call(
        functools.partial(update_kernel, na, ny, nz),
        out_shape=(jax.ShapeDtypeStruct((2 * K, STACK), jnp.bfloat16),
                   jax.ShapeDtypeStruct((1, K), jnp.float32),
                   jax.ShapeDtypeStruct((STACK, cols), jnp.bfloat16)),
        in_specs=[hbm, hbm, hbm],
        out_specs=(vmem, vmem, vmem),
        scratch_shapes=[
            pltpu.VMEM((K, cols), jnp.float32),
            pltpu.VMEM((NEW, cols), jnp.float32),
            slots(2, 2), slots(2), slots(2),
            slots(ny * nz), slots(na // 2), slots(na // 2), slots(ny * nz), slots(2), slots(2, 2),
            pltpu.VMEM((1, K), jnp.float32),
            pltpu.SemaphoreType.DMA,
            pltpu.SemaphoreType.DMA((2, cols // LOAD)),
            pltpu.SemaphoreType.DMA((6,)),
            pltpu.SemaphoreType.DMA((6,)),
        ],
        compiler_params=pltpu.CompilerParams(
            collective_id=0, has_side_effects=True, vmem_limit_bytes=32 * 1024 * 1024),
        name="pod_update",
    )(*(pltpu.with_memory_space_constraint(value, pltpu.HBM)
        for value in (basis, sigma.reshape(1, K), snapshots)))
    modes, values = pl.pallas_call(
        finish_kernel,
        out_shape=(jax.ShapeDtypeStruct((K, cols), jnp.float32),
                   jax.ShapeDtypeStruct((1, K), jnp.float32)),
        in_specs=[vmem, vmem, vmem],
        out_specs=(hbm, hbm),
        scratch_shapes=[pltpu.VMEM((K, cols), jnp.float32), pltpu.SemaphoreType.DMA((cols // CHUNK + 1,))],
        compiler_params=pltpu.CompilerParams(vmem_limit_bytes=8 * 1024 * 1024),
        name="modes_product",
    )(left, values, split)
    return modes, values.reshape(K)


def solution(mesh):
    placed = (P(None, AXES), P(), P(None, AXES))
    return jax.shard_map(
        per_device, mesh=mesh, in_specs=placed, out_specs=(P(None, AXES), P()), check_vma=False)
```
